32 devices in a mesh: dp: 4 (over z), ctx: 8 (over y, x, core).
Axes of the slice: x: 2, y: 2, z: 4, core: 2. Of those that a mesh axis runs over, the one named last changes fastest.
Arguments:
- source_picture_sequence: bfloat16 [4, 32, 8, 8, 16, 128], P('dp', 'ctx'), may hold values from -6 to 6
- slot_assignment: int32 [32], replicated, may hold values from 0 to 31, as said below
- segment_piece_counts: int32 [4], replicated, may hold values from 1 to 16, 32 in all
- logit_scaling: float32 [4], replicated, may hold values from 1 to 16
- filter_tap_coefficients: bfloat16 [3456, 256], replicated, may hold values from -0.109375 to 0.109375
- triple_linear_matrix: bfloat16 [256, 768], replicated, may hold values from -0.375 to 0.375
- final_linear_matrix: bfloat16 [256, 256], replicated, may hold values from -0.375 to 0.375
- upstream_gradient: bfloat16 [4, 32, 4, 128, 256], P('dp', 'ctx'), may hold values from -6 to 6
Outputs:
- latents: bfloat16 [4, 32, 4, 128, 256], P('dp', 'ctx')
- conv_grad: float32 [3456, 256], P('ctx')
The draws below stay inside these ranges and needn't reach their ends.
Inputs may be any that keep to these rules, and one draw needn't show every extreme that they name: `slot_assignment`: A permutation of the span numbers; entry i names the span at slot i, held by device i // 4. Each quarter of the span numbers, in order, fills one of the 4 positions on every device. The spans that follow one device's spans lie on at most two devices, at most two on any one device, and so do the spans that precede them; in every draw some device has two spans followed by spans on one other device.
All inputs are finite; a program needn't handle non-finite values.
Results may differ from the reference program's by a relative error of at most 0.0058.
Values may be sent and summed in bfloat16 or wider, within the bound.
No kernel may reach another device: no remote copies, remote signals or barrier semaphores. Data moves between devices by JAX's collectives and lax.ppermute only.
A program may use at most 128 MiB of HBM per device.

```python
import math
import jax
import jax.numpy as jnp
import numpy as np
from jax import lax

C_IN = 128
C_OUT = 256
SLOTS = 4
FRAME_ROWS = 8
FRAME_COLS = 16
CLIP_MOST = 16
SPANS = 32
CLIPS = 4
CELLS = 128
PATCH = 3456
HEADS = 4
GROUPS = 4


def draw_slot_assignment(key, part):
    device_total = SPANS // SLOTS
    device_order = jax.random.permutation(key, device_total).astype(jnp.int32)
    position = jnp.argsort(device_order).astype(jnp.int32)
    reverse_position = device_total - 1 - position
    table = jnp.stack([position, device_total + position, 2 * device_total + reverse_position, 3 * device_total + reverse_position], axis=1)
    return table.reshape(-1).astype(jnp.int32)


def draw_logit_scaling(key, part):
    return jnp.exp(jax.random.uniform(key, (HEADS,), jnp.float32, math.log(1.0), math.log(12.0)))


def shard_levels(rng, dims, shards, smallest, top_value):
    def one(axis_at, shards_of):
        heights = jax.random.uniform(jax.random.fold_in(jax.random.fold_in(rng, 6), axis_at), (shards_of,), jnp.float32, smallest / len(shards), top_value / len(shards))
        return jnp.repeat(jnp.exp(heights), dims[axis_at] // shards_of).reshape((-1,) + (1,) * (len(dims) - axis_at - 1))

    gain = one(*shards[0])
    for cut in shards[1:]:
        gain = gain * one(*cut)
    return gain


def split_up(amount, total, limit, slope):
    loads = [(1 << 20) // math.isqrt(grade ** slope) + 1 for grade in range(2, amount + 1)]
    rest, holding = total - limit - (amount - 1), [1] * (amount - 1)
    while rest > 0:
        candidates = [i for i in range(amount - 1) if holding[i] < limit]
        mass, remaining = sum([loads[i] for i in candidates]), rest
        for i in candidates:
            extra = min(limit - holding[i], max(1, remaining * loads[i] // mass), rest)
            holding[i] = holding[i] + extra
            rest = rest - extra
    return np.array([limit] + holding)


def ragged_sizes(stream_key, number_of, total, most, skew):
    if number_of == 2:
        one = jax.random.randint(stream_key, (), max(1, total - most), min(most, total - 1) + 1)
        return jnp.stack([one, total - one])
    lengths = jnp.asarray(split_up(number_of, total, most, skew), jnp.int32)
    pairs = (number_of - 1) // 2
    source_of, sink = lengths[1:1 + 2 * pairs:2], lengths[2:2 + 2 * pairs:2]
    slack = jnp.minimum(source_of - 1, most - sink)
    shifted = jax.random.randint(jax.random.fold_in(stream_key, 1), (pairs,), 0, 1 << 20) % (slack + 1)
    lengths = lengths.at[1:1 + 2 * pairs:2].set(source_of - shifted).at[2:2 + 2 * pairs:2].set(sink + shifted)
    return lengths[jax.random.permutation(jax.random.fold_in(stream_key, 2), number_of)]


def centred(own_key, extent, width, reach, cuts=(), held_as=jnp.bfloat16):
    result = width * jax.random.normal(own_key, extent, jnp.float32)
    if cuts:
        result = result * shard_levels(own_key, extent, cuts, -0.22, 0.18)
    return jnp.clip(result, -reach, reach).astype(held_as)


def setup_inputs(seed: int = 0) -> dict:
    key_list = jax.random.split(jax.random.key(seed), 9)
    source_picture_sequence = centred(key_list[0], (GROUPS, SPANS, 8, FRAME_ROWS, FRAME_COLS, C_IN), 1.0, 6.0, ((0, 4), (1, 8)))
    slot_assignment = draw_slot_assignment(jax.random.fold_in(key_list[8], 71), 0)
    segment_piece_counts = ragged_sizes(key_list[2], CLIPS, SPANS, CLIP_MOST, 2).astype(jnp.int32)
    logit_scaling = draw_logit_scaling(jax.random.fold_in(key_list[8], 71), 0)
    filter_tap_coefficients = centred(key_list[4], (PATCH, C_OUT), PATCH ** -0.5, 0.109375)
    triple_linear_matrix = centred(key_list[5], (C_OUT, 3 * C_OUT), C_OUT ** -0.5, 0.375)
    final_linear_matrix = centred(key_list[6], (C_OUT, C_OUT), C_OUT ** -0.5, 0.375)
    upstream_gradient = centred(key_list[7], (GROUPS, SPANS, 4, CELLS, C_OUT), 1.0, 6.0, ((0, 4), (1, 8)))
    return {"source_picture_sequence": source_picture_sequence, "slot_assignment": slot_assignment, "segment_piece_counts": segment_piece_counts, "logit_scaling": logit_scaling, "filter_tap_coefficients": filter_tap_coefficients, "triple_linear_matrix": triple_linear_matrix, "final_linear_matrix": final_linear_matrix, "upstream_gradient": upstream_gradient}


masked_score = -1e+30

def clip_marks(segment_piece_counts, span_ids):
    clip_ends = jnp.cumsum(segment_piece_counts, dtype=jnp.int32)
    clip_starts = clip_ends - segment_piece_counts
    clip_index = lax.optimization_barrier(jnp.sum((span_ids[:, None] >= clip_ends[None, :]).astype(jnp.int32), axis=1, dtype=jnp.int32))
    opening = jnp.any(span_ids[:, None] == clip_starts[None, :], axis=1)
    return (clip_index, opening)

def conv_patches(frames):
    span_total, unused_len, rows_h, cols_w, channel_in = frames.shape
    padded = jnp.pad(frames, ((0, 0), (0, 0), (1, 1), (1, 1), (0, 0)))
    tap_list = []
    for step_t in range(3):
        for step_h in range(3):
            for step_w in range(3):
                tap_list.append(padded[:, step_t:step_t + 7:2, step_h:step_h + rows_h, step_w:step_w + cols_w, :])
    return jnp.concatenate(tap_list, axis=-1).reshape(-1, 27 * channel_in)

def timewise_softmax_mixing(grid_tile_entries, logit_scaling, triple_linear_matrix, final_linear_matrix, allowance_pattern):
    channel_width = grid_tile_entries.shape[-1]
    channel_group_index = logit_scaling.shape[0]
    head_size = channel_width // channel_group_index
    values32 = grid_tile_entries.astype(jnp.float32)
    normed = (values32 * lax.rsqrt(lax.optimization_barrier(jnp.mean(values32 * values32, axis=-1, keepdims=True)) + 1e-06)).astype(jnp.bfloat16)
    projected = jnp.einsum('gac,cd->gad', normed.astype(jnp.float32), triple_linear_matrix.astype(jnp.float32))
    head_shape = grid_tile_entries.shape[:2] + (channel_group_index, head_size)
    queries = projected[..., :channel_width].reshape(head_shape)
    keys_all = projected[..., channel_width:2 * channel_width].reshape(head_shape)
    head_values = projected[..., 2 * channel_width:].reshape(head_shape).astype(jnp.bfloat16)
    queries = queries * lax.rsqrt(lax.optimization_barrier(jnp.sum(queries * queries, axis=-1, keepdims=True)) + 1e-06)
    keys_all = keys_all * lax.rsqrt(lax.optimization_barrier(jnp.sum(keys_all * keys_all, axis=-1, keepdims=True)) + 1e-06)
    affinity_logits = jnp.einsum('gahd,gbhd->ghab', queries, keys_all, precision=lax.Precision.HIGHEST)
    affinity_logits = affinity_logits * logit_scaling[None, :, None, None]
    affinity_logits = jnp.where(allowance_pattern[None, None], affinity_logits, masked_score)
    highest = lax.optimization_barrier(jnp.max(affinity_logits, axis=-1, keepdims=True))
    weights = jnp.exp(affinity_logits - highest)
    probabilities = (weights / lax.optimization_barrier(jnp.sum(weights, axis=-1, keepdims=True))).astype(jnp.bfloat16)
    mixed_heads = jnp.einsum('ghab,gbhd->gahd', probabilities.astype(jnp.float32), head_values.astype(jnp.float32))
    mixed_heads = mixed_heads.astype(jnp.bfloat16).reshape(grid_tile_entries.shape)
    branch = jnp.einsum('gac,cd->gad', mixed_heads.astype(jnp.float32), final_linear_matrix.astype(jnp.float32))
    return (values32 + branch).astype(jnp.bfloat16)

def reference(source_picture_sequence, slot_assignment, segment_piece_counts, logit_scaling, filter_tap_coefficients, triple_linear_matrix, final_linear_matrix, upstream_gradient):
    span_ids = jnp.arange(SPANS, dtype=jnp.int32)
    clip_index, opening = clip_marks(segment_piece_counts, span_ids)
    slot_of_span = jnp.argsort(slot_assignment).astype(jnp.int32)
    frame_clip = jnp.repeat(clip_index, 4)
    frame_time = jnp.arange(SPANS * 4, dtype=jnp.int32)
    allowance_pattern = (frame_clip[:, None] == frame_clip[None, :]) & (frame_time[None, :] <= frame_time[:, None])
    conv_grad = jnp.zeros((PATCH, C_OUT), jnp.float32)
    results = []
    for group_idx in range(GROUPS):
        span_order = source_picture_sequence[group_idx][slot_of_span]
        previous = jnp.concatenate([jnp.zeros_like(span_order[:1, 6:]), span_order[:-1, 6:]], axis=0)
        previous = jnp.where(opening[:, None, None, None, None], jnp.zeros_like(previous), previous)
        patches = conv_patches(jnp.concatenate([previous, span_order], axis=1))
        conv_out = jnp.dot(patches, filter_tap_coefficients, preferred_element_type=jnp.float32).astype(jnp.bfloat16)
        grad_rows = upstream_gradient[group_idx][slot_of_span].reshape(-1, C_OUT)
        conv_grad = conv_grad + jnp.dot(patches.T, grad_rows, preferred_element_type=jnp.float32)
        location_entry_count = jnp.transpose(conv_out.reshape(SPANS * 4, CELLS, C_OUT), (1, 0, 2))
        blended_result = lax.map(lambda grid_tile_entries: timewise_softmax_mixing(grid_tile_entries[None], logit_scaling, triple_linear_matrix, final_linear_matrix, allowance_pattern)[0], location_entry_count)
        latent_spans = jnp.transpose(blended_result, (1, 0, 2)).reshape(SPANS, 4, CELLS, C_OUT)
        results.append(latent_spans[slot_assignment])
    return (jnp.stack(results), conv_grad)
```

```python
import functools

import jax
import jax.numpy as jnp
from jax import lax
from jax.experimental import pallas as pl
from jax.experimental.pallas import tpu as pltpu
from jax.sharding import PartitionSpec as P

BF = jnp.bfloat16
F32 = jnp.float32
VMEM_LIMIT = 56 * 1024 * 1024
ROWS, COLS, CIN, COUT = 8, 16, 128, 256
SLOTS, STEPS = 4, 4
FRAMES = SLOTS * STEPS
TAPS = [(h, w) for h in range(3) for w in range(3)]
TAP_SETS = [TAPS[0:2], TAPS[2:4], TAPS[4:6], TAPS[6:8], TAPS[8:9]]


def iota(shape, axis):
    return lax.broadcasted_iota(jnp.int32, shape, axis)


def dot(a, b):
    return jnp.dot(a, b, preferred_element_type=F32)


def dot_t(a, b):
    return lax.dot_general(a, b, (((1,), (1,)), ((), ())), preferred_element_type=F32)


def swap_matrix(outer, inner):
    total = outer * inner
    i, j = iota((total, total), 0), iota((total, total), 1)
    return ((i % outer == j // inner) & (i // outer == j % inner)).astype(F32).astype(BF)


def params(**kw):
    return pltpu.CompilerParams(vmem_limit_bytes=VMEM_LIMIT, **kw)


def cost(flops, nbytes):
    return pl.CostEstimate(flops=flops, bytes_accessed=nbytes, transcendentals=0)


VMEM = pl.BlockSpec(memory_space=pltpu.VMEM)
SMEM = pl.BlockSpec(memory_space=pltpu.SMEM)


def fill_slots(assign, slot_of):
    def body(i, carry):
        slot_of[assign[i]] = i
        return carry

    lax.fori_loop(0, assign.shape[0], body, 0)


def is_opening(span, counts):
    start, found = jnp.int32(0), jnp.int32(0)
    for k in range(counts.shape[0]):
        found = jnp.where(span == start, jnp.int32(1), found)
        start = start + counts[k]
    return found


def lay_out_taps(x_ref, prev, padded):
    padded[...] = jnp.zeros_like(padded)
    swap = swap_matrix(FRAMES, COLS)

    def tile(s, f, r):
        return x_ref[s, f, r] if f >= 0 else prev(s, f, r)

    for r in range(0, ROWS, 2):
        for kt in range(3):
            cols = [
                jnp.concatenate([tile(s, 2 * t - 2 + kt, rr) for s in range(SLOTS) for t in range(STEPS)], axis=0)
                for rr in (r, r + 1)
            ]
            turned = dot(swap, jnp.concatenate(cols, axis=1)).astype(BF)
            for n in range(2):
                part = turned[:, n * CIN : (n + 1) * CIN].reshape(COLS, FRAMES, CIN)
                padded[r + n + 1, 1 : COLS + 1, :, kt * CIN : (kt + 1) * CIN] = part


def tap_block(padded, taps):
    blocks = [padded[h : h + ROWS, w : w + COLS].reshape(ROWS * COLS * FRAMES, 3 * CIN) for h, w in taps]
    return blocks[0] if len(blocks) == 1 else jnp.concatenate(blocks, axis=1)


def tap_rows(kt, h, w):
    at = ((kt * 3 + h) * 3 + w) * CIN
    return slice(at, at + CIN)


def conv_kernel(cells, x_ref, w_ref, out_ref, padded, edge):
    lay_out_taps(x_ref, lambda s, f, r: jnp.zeros((COLS, CIN), BF), padded)
    total = None
    for taps in TAP_SETS:
        rows = jnp.concatenate([w_ref[tap_rows(kt, h, w), :] for h, w in taps for kt in range(3)], axis=0)
        term = dot(tap_block(padded, taps), rows)
        total = term if total is None else total + term
    main = cells * FRAMES
    out_ref[:, :main, :] = total.astype(BF).reshape(out_ref.shape[0], main, COUT)
    wide = SLOTS * COLS
    i, j = iota((3 * wide, wide), 0), iota((3 * wide, wide), 1)
    k = i % wide
    q = (k // (SLOTS * cells)) * cells + k % cells
    s = (k // cells) % SLOTS
    shift = ((j // COLS == s) & (j % COLS == q + i // wide - 1)).astype(F32).astype(BF)
    edge[0] = jnp.zeros_like(edge[0])
    edge[ROWS + 1] = jnp.zeros_like(edge[0])
    for r in range(ROWS):
        tails = jnp.concatenate(
            [jnp.concatenate([x_ref[s, f, r] for s in range(SLOTS)], axis=0) for f in (6, 7)], axis=1
        )
        edge[r + 1] = dot(shift, tails).astype(BF)
    carry = None
    for h, w in TAPS:
        rows = jnp.concatenate([w_ref[tap_rows(kt, h, w), :] for kt in range(2)], axis=0)
        part = edge[h : h + ROWS, w * wide : (w + 1) * wide, :].reshape(ROWS * wide, 2 * CIN)
        term = dot(part, rows)
        carry = term if carry is None else carry + term
    out_ref[:, main:, :] = carry.astype(BF).reshape(out_ref.shape[0], SLOTS * cells, COUT)


def run_conv(frames, taps, ctx):
    cells = ROWS * COLS // ctx
    return pl.pallas_call(
        functools.partial(conv_kernel, cells),
        out_shape=jax.ShapeDtypeStruct((ctx, cells * (FRAMES + SLOTS), COUT), BF),
        in_specs=[VMEM, VMEM],
        out_specs=VMEM,
        scratch_shapes=[
            pltpu.VMEM((ROWS + 2, COLS + 2, FRAMES, 3 * CIN), BF),
            pltpu.VMEM((ROWS + 2, 3 * SLOTS * COLS, 2 * CIN), BF),
        ],
        compiler_params=params(),
        cost_estimate=cost(4_800_000_000, 4_000_000),
        name="conv_forward",
    )(frames, taps)


def tails_kernel(assign, me_ref, x_ref, out_ref, slot_of):
    fill_slots(assign, slot_of)
    me = me_ref[0]
    owners = []
    for p in range(SLOTS):
        after = assign[me * SLOTS + p] + 1
        known = after < assign.shape[0]
        owner = jnp.where(known, slot_of[jnp.where(known, after, 0)] // SLOTS, -1)
        place = jnp.int32(0)
        for earlier in owners:
            place = place + (earlier == owner).astype(jnp.int32)
        owners.append(owner)

        @pl.when(known)
        def _():
            out_ref[jnp.maximum(owner, 0), jnp.minimum(place, 1)] = x_ref[p]


def run_tails(frames, assign, me, ctx):
    shape = (SLOTS, 2, ROWS, COLS, CIN)
    return pl.pallas_call(
        tails_kernel,
        grid=(1,),
        out_shape=jax.ShapeDtypeStruct((ctx, 2) + shape[1:], BF),
        in_specs=[SMEM, SMEM, pl.BlockSpec(shape, lambda i: (0, 3, 0, 0, 0))],
        out_specs=pl.BlockSpec((ctx, 2) + shape[1:], lambda i: (0, 0, 0, 0, 0, 0)),
        scratch_shapes=[pltpu.SMEM(assign.shape, jnp.int32)],
        compiler_params=params(),
        cost_estimate=cost(0, 2_000_000),
        name="send_tails",
    )(assign, me, frames)


def grad_kernel(assign, counts, me_ref, x_ref, u_ref, tails_ref, keep_ref, send_ref, slot_of, padded, turned, whole):
    fill_slots(assign, slot_of)
    me = me_ref[0]
    found = []
    for i in range(SLOTS):
        span = assign[me * SLOTS + i]
        opening = is_opening(span, counts)
        slot = slot_of[jnp.maximum(span - 1, 0)]
        owner = slot // SLOTS
        place = jnp.int32(0)
        for p in range(SLOTS):
            after = assign[owner * SLOTS + p] + 1
            known = after < assign.shape[0]
            same = known & (slot_of[jnp.where(known, after, 0)] // SLOTS == me) & (p < slot % SLOTS)
            place = place + same.astype(jnp.int32)
        found.append((owner, jnp.minimum(place, 1), opening))

    def prev(s, f, r):
        owner, place, opening = found[s]
        got = tails_ref[owner, place, f + 2, r]
        return jnp.where(opening > 0, jnp.zeros_like(got), got)

    lay_out_taps(x_ref, prev, padded)
    swap = swap_matrix(FRAMES, COLS)
    span_rows = COLS * FRAMES
    for r in range(ROWS):
        block = jnp.concatenate(
            [u_ref[s, t, r * COLS : (r + 1) * COLS, :] for s in range(SLOTS) for t in range(STEPS)], axis=0
        )
        turned[:, r * span_rows : (r + 1) * span_rows] = dot(swap, block).T.astype(BF)
    for taps in TAP_SETS:
        product = dot(turned[...], tap_block(padded, taps)).T
        for n, (h, w) in enumerate(taps):
            for kt in range(3):
                at = (n * 3 + kt) * CIN
                whole[tap_rows(kt, h, w), :] = product[at : at + CIN, :]
    core = me % 2
    rows = keep_ref.shape[1]
    for i in range(keep_ref.shape[0]):
        keep_ref[i] = whole[pl.ds(pl.multiple_of((2 * i + core) * rows, 16), rows), :]
        send_ref[i] = whole[pl.ds(pl.multiple_of((2 * i + 1 - core) * rows, 16), rows), :].astype(BF)


def run_grad(assign, counts, me, frames, upstream, tails, ctx):
    patch = 27 * CIN
    half = (ctx // 2, patch // ctx, COUT)
    return pl.pallas_call(
        grad_kernel,
        out_shape=(jax.ShapeDtypeStruct(half, F32), jax.ShapeDtypeStruct(half, BF)),
        in_specs=[SMEM, SMEM, SMEM, VMEM, VMEM, VMEM],
        out_specs=(VMEM, VMEM),
        scratch_shapes=[
            pltpu.SMEM(assign.shape, jnp.int32),
            pltpu.VMEM((ROWS + 2, COLS + 2, FRAMES, 3 * CIN), BF),
            pltpu.VMEM((COUT, ROWS * COLS * FRAMES), BF),
            pltpu.VMEM((patch, COUT), F32),
        ],
        compiler_params=params(),
        cost_estimate=cost(4_000_000_000, 6_000_000),
        name="conv_gradient",
    )(assign, counts, me, frames, upstream, tails)


def attend_kernel(cells, assign, counts, scale, got_ref, qkv_ref, last_ref, out_ref, slot_of, rows_of, q_ref, k_ref, v_ref, bias):
    ctx = got_ref.shape[0]
    main = cells * FRAMES
    total = ctx * FRAMES
    fill_slots(assign, slot_of)

    def mark(shape, axis):
        spot = iota(shape, axis)
        span = jnp.zeros(shape, jnp.int32)
        for i in range(ctx * SLOTS):
            span = jnp.where(spot // STEPS == i, assign[i], span)
        clip, end = jnp.zeros(shape, jnp.int32), jnp.int32(0)
        for k in range(counts.shape[0]):
            end = end + counts[k]
            clip = clip + (span >= end).astype(jnp.int32)
        return span * STEPS + spot % STEPS, clip

    time_b, clip_b = mark((1, total), 1)
    time_a, clip_a = mark((total, 1), 0)
    allowed = (clip_a == clip_b) & (time_b <= time_a)
    bias[...] = jnp.where(allowed, 0.0, -1e30)

    i, j = iota((main, main), 0), iota((main, main), 1)
    held = j // (SLOTS * cells)
    fits = (i % STEPS == 0) & ((i // STEPS) % SLOTS == held) & (i // FRAMES == j % cells)
    base = jnp.where(fits, 1, 0)
    lane = iota((1, main), 1)
    from_slot = (lane // cells) % SLOTS
    lane_held = lane // (SLOTS * cells)
    same_head = (iota((COUT, COUT), 0) // 64 == iota((COUT, COUT), 1) // 64).astype(F32).astype(BF)
    head = iota((1, COUT), 1) // 64
    gain = jnp.zeros((1, COUT), F32)
    for h in range(COUT // 64):
        gain = jnp.where(head == h, scale[h], gain)

    def project(src, carry):
        pick = jnp.full((1, main), -1, jnp.int32)
        blocks = []
        for s in range(SLOTS):
            span = assign[src * SLOTS + s]
            slot = slot_of[jnp.maximum(span - 1, 0)]
            spot = jnp.where(is_opening(span, counts) > 0, -1, slot % SLOTS)
            pick = jnp.where(lane_held == s, spot, pick)
            blocks.append(got_ref[slot // SLOTS, main:, :])
        chosen = jnp.where(pick == from_slot, base, 0).astype(F32).astype(BF)
        value = got_ref[src, :main, :].astype(F32) + dot(chosen, jnp.concatenate(blocks, axis=0))
        value = value.astype(BF)
        rows_of[src] = value.reshape(cells, FRAMES, COUT)
        value = value.astype(F32)
        normed = value * lax.rsqrt(jnp.mean(value * value, axis=-1, keepdims=True) + 1e-6)
        mapped = dot(normed.astype(BF), qkv_ref[...])
        query, key = mapped[:, :COUT], mapped[:, COUT : 2 * COUT]
        query = query * (lax.rsqrt(dot((query * query).astype(BF), same_head) + 1e-6) * gain)
        key = key * lax.rsqrt(dot((key * key).astype(BF), same_head) + 1e-6)
        q_ref[src] = query.astype(BF).reshape(cells, FRAMES, COUT)
        k_ref[src] = key.astype(BF).reshape(cells, FRAMES, COUT)
        v_ref[src] = mapped[:, 2 * COUT :].astype(BF).reshape(cells, FRAMES, COUT)
        return carry

    lax.fori_loop(0, ctx, project, 0)

    low = iota((1, 128), 1) < 64
    ones = [jnp.where(low, 1.0, 0.0), jnp.where(low, 0.0, 1.0)]
    block = min(128, total)

    def mix(cell, carry):
        for pair in range(2):
            lanes = slice(pair * 128, (pair + 1) * 128)
            key = k_ref[:, cell, :, lanes].reshape(total, 128)
            value = v_ref[:, cell, :, lanes].reshape(total, 128)
            zero = jnp.zeros_like(key)
            keys = jnp.concatenate([jnp.where(low, key, zero), jnp.where(low, zero, key)], axis=0)
            sides = [jnp.where(low, value, zero), jnp.where(low, zero, value)]
            flags = [jnp.broadcast_to(ones[n].astype(BF), (total, 128)) for n in range(2)]
            values = jnp.concatenate(
                [jnp.concatenate([sides[n], flags[n]], axis=1) for n in range(2)], axis=0
            )
            for at in range(0, total, block):
                part = slice(at // FRAMES, (at + block) // FRAMES)
                query = q_ref[part, cell, :, lanes].reshape(block, 128)
                logits = dot_t(query, keys)
                mask = bias[at : at + block, :]
                weights = jnp.exp(logits + jnp.concatenate([mask, mask], axis=1)).astype(BF)
                sums = dot(weights, values)
                mixed = (sums[:, :128] / sums[:, 128:]).astype(BF)
                q_ref[part, cell, :, lanes] = mixed.reshape(block // FRAMES, FRAMES, 128)
        return carry

    lax.fori_loop(0, cells, mix, 0)

    turn = swap_matrix(cells, FRAMES)

    def finish(src, carry):
        mixed = q_ref[src].reshape(main, COUT)
        value = rows_of[src].reshape(main, COUT).astype(F32)
        latent = (value + dot(mixed, last_ref[...])).astype(BF)
        out_ref[src] = dot(turn, latent).astype(BF)
        return carry

    lax.fori_loop(0, ctx, finish, 0)


def run_attend(assign, counts, scale, got, qkv, last, ctx):
    cells = ROWS * COLS // ctx
    total = ctx * FRAMES
    held = pltpu.VMEM((ctx, cells, FRAMES, COUT), BF)
    return pl.pallas_call(
        functools.partial(attend_kernel, cells),
        out_shape=jax.ShapeDtypeStruct((ctx, cells * FRAMES, COUT), BF),
        in_specs=[SMEM, SMEM, SMEM, VMEM, VMEM, VMEM],
        out_specs=VMEM,
        scratch_shapes=[pltpu.SMEM(assign.shape, jnp.int32), held, held, held, held, pltpu.VMEM((total, total), F32)],
        compiler_params=params(),
        cost_estimate=cost(3_000_000_000, 4_000_000),
        name="attend",
    )(assign, counts, scale, got, qkv, last)


def fold_kernel(me_ref, keep_ref, got_ref, own_ref, *send_refs):
    mine = me_ref[0] // 2
    own_ref[...] = keep_ref[mine] + got_ref[mine].astype(F32)
    for k, ref in enumerate(send_refs):
        other = mine ^ (k + 1)
        ref[...] = (keep_ref[other] + got_ref[other].astype(F32)).astype(BF)


def run_fold(me, keep, got, ctx):
    piece = keep.shape[1:]
    peers = ctx // 2 - 1
    return pl.pallas_call(
        fold_kernel,
        out_shape=(jax.ShapeDtypeStruct(piece, F32),) + (jax.ShapeDtypeStruct(piece, BF),) * peers,
        in_specs=[SMEM, VMEM, VMEM],
        out_specs=(VMEM,) * (peers + 1),
        compiler_params=params(),
        cost_estimate=cost(0, 4_000_000),
        name="fold_cores",
    )(me, keep, got)


def add_kernel(own_ref, *refs):
    total = own_ref[...].astype(F32)
    for ref in refs[:-1]:
        total = total + ref[...].astype(F32)
    refs[-1][...] = total.astype(refs[-1].dtype)


def run_add(own, others, dtype):
    return pl.pallas_call(
        add_kernel,
        out_shape=jax.ShapeDtypeStruct(own.shape, dtype),
        in_specs=[VMEM] * (1 + len(others)),
        out_specs=VMEM,
        compiler_params=params(),
        cost_estimate=cost(0, 1_000_000),
        name="add_parts",
    )(own, *others)


def flip(value, axis, size, bits):
    return lax.ppermute(value, axis, [(i, i ^ bits) for i in range(size)])


def per_device(ctx, dp, frames, assign, counts, scale, taps, qkv, last, upstream):
    me = lax.axis_index("ctx").astype(jnp.int32).reshape(1)
    frames, upstream = frames[0], upstream[0]
    cells = ROWS * COLS // ctx
    tails = lax.all_to_all(run_tails(frames, assign, me, ctx), "ctx", 0, 0, tiled=True)
    sent = run_conv(frames, taps, ctx)
    got = lax.all_to_all(sent, "ctx", 0, 0, tiled=True)

    keep, send = run_grad(assign, counts, me, frames, upstream, tails, ctx)
    own, *parts = run_fold(me, keep, flip(send, "ctx", ctx, 1), ctx)
    share = run_add(own, [flip(part, "ctx", ctx, 2 * (k + 1)) for k, part in enumerate(parts)], BF)
    bits = 1
    while bits < dp:
        share = run_add(share, [flip(share, "dp", dp, bits)], BF if bits * 2 < dp else F32)
        bits *= 2

    blended = run_attend(assign, counts, scale, got, qkv, last, ctx)
    back = lax.all_to_all(blended, "ctx", 0, 0, tiled=True)
    latents = back.reshape(ctx, SLOTS, STEPS, cells, COUT).transpose(1, 2, 0, 3, 4)
    return (latents.reshape(1, SLOTS, STEPS, ctx * cells, COUT), share)


def solution(mesh):
    placed = (
        P("dp", "ctx", None, None, None, None),
        P(),
        P(),
        P(),
        P(),
        P(),
        P(),
        P("dp", "ctx", None, None, None),
    )
    return jax.shard_map(
        functools.partial(per_device, mesh.shape["ctx"], mesh.shape["dp"]),
        mesh=mesh,
        in_specs=placed,
        out_specs=(P("dp", "ctx", None, None, None), P("ctx", None)),
        check_vma=False,
    )
```

```python
import functools

import jax
import jax.numpy as jnp
from jax import lax
from jax.experimental import pallas as pl
from jax.experimental.pallas import tpu as pltpu
from jax.sharding import PartitionSpec as P

BF = jnp.bfloat16
F32 = jnp.float32
VMEM_LIMIT = 56 * 1024 * 1024
ROWS, COLS, CIN, COUT = 8, 16, 128, 256
SLOTS, STEPS = 4, 4
FRAMES = SLOTS * STEPS
TAPS = [(h, w) for h in range(3) for w in range(3)]
TAP_SETS = [TAPS[0:2], TAPS[2:4], TAPS[4:6], TAPS[6:8], TAPS[8:9]]


def iota(shape, axis):
    return lax.broadcasted_iota(jnp.int32, shape, axis)


def dot(a, b):
    return jnp.dot(a, b, preferred_element_type=F32)


def dot_t(a, b):
    return lax.dot_general(a, b, (((1,), (1,)), ((), ())), preferred_element_type=F32)


def swap_matrix(outer, inner):
    total = outer * inner
    i, j = iota((total, total), 0), iota((total, total), 1)
    return ((i % outer == j // inner) & (i // outer == j % inner)).astype(F32).astype(BF)


def params(**kw):
    return pltpu.CompilerParams(vmem_limit_bytes=VMEM_LIMIT, **kw)


def cost(flops, nbytes):
    return pl.CostEstimate(flops=flops, bytes_accessed=nbytes, transcendentals=0)


VMEM = pl.BlockSpec(memory_space=pltpu.VMEM)
SMEM = pl.BlockSpec(memory_space=pltpu.SMEM)
ANY = pl.BlockSpec(memory_space=pl.ANY)


def fill_slots(assign, slot_of):
    def body(i, carry):
        slot_of[assign[i]] = i
        return carry

    lax.fori_loop(0, assign.shape[0], body, 0)


def is_opening(span, counts):
    start, found = jnp.int32(0), jnp.int32(0)
    for k in range(counts.shape[0]):
        found = jnp.where(span == start, jnp.int32(1), found)
        start = start + counts[k]
    return found


def lay_out_taps(x_ref, prev, padded):
    padded[...] = jnp.zeros_like(padded)
    swap = swap_matrix(FRAMES, COLS)

    def tile(s, f, r):
        return x_ref[s, f, r] if f >= 0 else prev(s, f, r)

    for r in range(0, ROWS, 2):
        for kt in range(3):
            cols = [
                jnp.concatenate([tile(s, 2 * t - 2 + kt, rr) for s in range(SLOTS) for t in range(STEPS)], axis=0)
                for rr in (r, r + 1)
            ]
            turned = dot(swap, jnp.concatenate(cols, axis=1)).astype(BF)
            for n in range(2):
                part = turned[:, n * CIN : (n + 1) * CIN].reshape(COLS, FRAMES, CIN)
                padded[r + n + 1, 1 : COLS + 1, :, kt * CIN : (kt + 1) * CIN] = part


def tap_block(padded, taps):
    blocks = [padded[h : h + ROWS, w : w + COLS].reshape(ROWS * COLS * FRAMES, 3 * CIN) for h, w in taps]
    return blocks[0] if len(blocks) == 1 else jnp.concatenate(blocks, axis=1)


def tap_rows(kt, h, w):
    at = ((kt * 3 + h) * 3 + w) * CIN
    return slice(at, at + CIN)


def device_at(me, chip_bits, core_bit):
    return me ^ (2 * chip_bits + core_bit)


def conv_kernel(cells, me_ref, x_ref, w_ref, *refs):
    out_refs, (main_part, edge_part, padded, edge) = refs[:-4], refs[-4:]
    lay_out_taps(x_ref, lambda s, f, r: jnp.zeros((COLS, CIN), BF), padded)
    total = None
    for taps in TAP_SETS:
        rows = jnp.concatenate([w_ref[tap_rows(kt, h, w), :] for h, w in taps for kt in range(3)], axis=0)
        term = dot(tap_block(padded, taps), rows)
        total = term if total is None else total + term
    main = cells * FRAMES
    main_part[...] = total.astype(BF).reshape(main_part.shape)
    wide = SLOTS * COLS
    i, j = iota((3 * wide, wide), 0), iota((3 * wide, wide), 1)
    k = i % wide
    q = (k // (SLOTS * cells)) * cells + k % cells
    s = (k // cells) % SLOTS
    shift = ((j // COLS == s) & (j % COLS == q + i // wide - 1)).astype(F32).astype(BF)
    edge[0] = jnp.zeros_like(edge[0])
    edge[ROWS + 1] = jnp.zeros_like(edge[0])
    for r in range(ROWS):
        tails = jnp.concatenate(
            [jnp.concatenate([x_ref[s, f, r] for s in range(SLOTS)], axis=0) for f in (6, 7)], axis=1
        )
        edge[r + 1] = dot(shift, tails).astype(BF)
    carry = None
    for h, w in TAPS:
        rows = jnp.concatenate([w_ref[tap_rows(kt, h, w), :] for kt in range(2)], axis=0)
        part = edge[h : h + ROWS, w * wide : (w + 1) * wide, :].reshape(ROWS * wide, 2 * CIN)
        term = dot(part, rows)
        carry = term if carry is None else carry + term
    edge_part[...] = carry.astype(BF).reshape(edge_part.shape)
    me = me_ref[0]
    for k, ref in enumerate(out_refs):
        for c in range(2):
            to = device_at(me, k, c)
            ref[c, :main, :] = main_part[to]
            ref[c, main:, :] = edge_part[to]


def run_conv(me, frames, taps, ctx):
    cells = ROWS * COLS // ctx
    return pl.pallas_call(
        functools.partial(conv_kernel, cells),
        out_shape=[jax.ShapeDtypeStruct((2, cells * (FRAMES + SLOTS), COUT), BF)] * (ctx // 2),
        in_specs=[SMEM, VMEM, VMEM],
        out_specs=[VMEM] * (ctx // 2),
        scratch_shapes=[
            pltpu.VMEM((ctx, cells * FRAMES, COUT), BF),
            pltpu.VMEM((ctx, cells * SLOTS, COUT), BF),
            pltpu.VMEM((ROWS + 2, COLS + 2, FRAMES, 3 * CIN), BF),
            pltpu.VMEM((ROWS + 2, 3 * SLOTS * COLS, 2 * CIN), BF),
        ],
        compiler_params=params(),
        cost_estimate=cost(4_800_000_000, 4_000_000),
        name="conv_forward",
    )(me, frames, taps)


def copy_kernel(x_ref, out_ref):
    out_ref[...] = x_ref[...]


def run_tails(frames):
    shape = (SLOTS, 2, ROWS, COLS, CIN)
    return pl.pallas_call(
        copy_kernel,
        grid=(1,),
        out_shape=jax.ShapeDtypeStruct(shape, BF),
        in_specs=[pl.BlockSpec(shape, lambda i: (0, 3, 0, 0, 0))],
        out_specs=pl.BlockSpec(shape, lambda i: (0, 0, 0, 0, 0)),
        compiler_params=params(),
        cost_estimate=cost(0, 500_000),
        name="cut_tails",
    )(frames)


def grad_kernel(chips, assign, counts, me_ref, x_ref, u_ref, unused_ref, *refs):
    tails, refs = refs[: 2 * chips], refs[2 * chips :]
    sends, keeps = refs[:chips], refs[chips : 2 * chips]
    slot_of, padded, turned, whole, before, sem = refs[2 * chips :]
    fill_slots(assign, slot_of)
    me = me_ref[0]
    openings = []
    for i in range(SLOTS):
        span = assign[me * SLOTS + i]
        openings.append(is_opening(span, counts))
        slot = slot_of[jnp.maximum(span - 1, 0)]
        apart = (slot // SLOTS) ^ me
        for n, ref in enumerate(tails):

            @pl.when(apart == n)
            def _():
                pltpu.make_async_copy(ref.at[slot % SLOTS], before.at[i], sem.at[i]).start()

    for i in range(SLOTS):
        pltpu.make_async_copy(tails[0].at[0], before.at[i], sem.at[i]).wait()

    def prev(s, f, r):
        got = before[s, f + 2, r]
        return jnp.where(openings[s] > 0, jnp.zeros_like(got), got)

    lay_out_taps(x_ref, prev, padded)
    swap = swap_matrix(FRAMES, COLS)
    span_rows = COLS * FRAMES
    for r in range(ROWS):
        block = jnp.concatenate(
            [u_ref[s, t, r * COLS : (r + 1) * COLS, :] for s in range(SLOTS) for t in range(STEPS)], axis=0
        )
        turned[:, r * span_rows : (r + 1) * span_rows] = dot(swap, block).T.astype(BF)
    for taps in TAP_SETS:
        product = dot(turned[...], tap_block(padded, taps)).T
        for n, (h, w) in enumerate(taps):
            for kt in range(3):
                at = (n * 3 + kt) * CIN
                whole[tap_rows(kt, h, w), :] = product[at : at + CIN, :]
    rows = keeps[0].shape[0]
    for k in range(chips):
        kept, sent = device_at(me, k, 0), device_at(me, k, 1)
        keeps[k][...] = whole[pl.ds(pl.multiple_of(kept * rows, 16), rows), :]
        sends[k][...] = whole[pl.ds(pl.multiple_of(sent * rows, 16), rows), :].astype(BF)


def run_grad(assign, counts, me, frames, upstream, after, tails, ctx):
    patch = 27 * CIN
    chips, rows = ctx // 2, patch // ctx
    return pl.pallas_call(
        functools.partial(grad_kernel, chips),
        out_shape=[jax.ShapeDtypeStruct((rows, COUT), dtype) for dtype in (BF, F32) for k in range(chips)],
        in_specs=[SMEM, SMEM, SMEM, VMEM, VMEM, ANY] + [ANY] * ctx,
        out_specs=[VMEM] * (2 * chips),
        scratch_shapes=[
            pltpu.SMEM(assign.shape, jnp.int32),
            pltpu.VMEM((ROWS + 2, COLS + 2, FRAMES, 3 * CIN), BF),
            pltpu.VMEM((COUT, ROWS * COLS * FRAMES), BF),
            pltpu.VMEM((patch, COUT), F32),
            pltpu.VMEM((SLOTS, 2, ROWS, COLS, CIN), BF),
            pltpu.SemaphoreType.DMA((SLOTS,)),
        ],
        compiler_params=params(),
        cost_estimate=cost(4_000_000_000, 6_000_000),
        name="conv_gradient",
    )(assign, counts, me, frames, upstream, after, *tails)


def attend_kernel(cells, ctx, assign, counts, scale, me_ref, qkv_ref, last_ref, *refs):
    chips = ctx // 2
    got_refs, out_refs = refs[:ctx], refs[ctx : ctx + chips]
    slot_of, rows_of, q_ref, k_ref, v_ref, edges, bias = refs[ctx + chips :]
    me = me_ref[0]
    main = cells * FRAMES
    total = ctx * FRAMES
    fill_slots(assign, slot_of)

    def mark(shape, axis):
        spot = iota(shape, axis)
        span = jnp.zeros(shape, jnp.int32)
        for i in range(ctx * SLOTS):
            span = jnp.where(spot // STEPS == i, assign[(me ^ (i // SLOTS)) * SLOTS + i % SLOTS], span)
        clip, end = jnp.zeros(shape, jnp.int32), jnp.int32(0)
        for k in range(counts.shape[0]):
            end = end + counts[k]
            clip = clip + (span >= end).astype(jnp.int32)
        return span * STEPS + spot % STEPS, clip

    time_b, clip_b = mark((1, total), 1)
    time_a, clip_a = mark((total, 1), 0)
    allowed = (clip_a == clip_b) & (time_b <= time_a)
    bias[...] = jnp.where(allowed, 0.0, -1e30)

    i, j = iota((main, main), 0), iota((main, main), 1)
    held = j // (SLOTS * cells)
    fits = (i % STEPS == 0) & ((i // STEPS) % SLOTS == held) & (i // FRAMES == j % cells)
    base = jnp.where(fits, 1, 0)
    lane = iota((1, main), 1)
    from_slot = (lane // cells) % SLOTS
    lane_held = lane // (SLOTS * cells)
    same_head = (iota((COUT, COUT), 0) // 64 == iota((COUT, COUT), 1) // 64).astype(F32).astype(BF)
    head = iota((1, COUT), 1) // 64
    gain = jnp.zeros((1, COUT), F32)
    for h in range(COUT // 64):
        gain = jnp.where(head == h, scale[h], gain)

    for src in range(ctx):
        edges[src] = got_refs[src][0, main:, :]
        rows_of[src] = got_refs[src][0, :main, :].reshape(cells, FRAMES, COUT)

    def project(src, carry):
        pick = jnp.full((1, main), -1, jnp.int32)
        blocks = []
        for s in range(SLOTS):
            span = assign[(me ^ src) * SLOTS + s]
            slot = slot_of[jnp.maximum(span - 1, 0)]
            spot = jnp.where(is_opening(span, counts) > 0, -1, slot % SLOTS)
            pick = jnp.where(lane_held == s, spot, pick)
            blocks.append(edges[(slot // SLOTS) ^ me])
        chosen = jnp.where(pick == from_slot, base, 0).astype(F32).astype(BF)
        value = rows_of[src].reshape(main, COUT).astype(F32) + dot(chosen, jnp.concatenate(blocks, axis=0))
        value = value.astype(BF)
        rows_of[src] = value.reshape(cells, FRAMES, COUT)
        value = value.astype(F32)
        normed = value * lax.rsqrt(jnp.mean(value * value, axis=-1, keepdims=True) + 1e-6)
        mapped = dot(normed.astype(BF), qkv_ref[...])
        query, key = mapped[:, :COUT], mapped[:, COUT : 2 * COUT]
        query = query * (lax.rsqrt(dot((query * query).astype(BF), same_head) + 1e-6) * gain)
        key = key * lax.rsqrt(dot((key * key).astype(BF), same_head) + 1e-6)
        q_ref[src] = query.astype(BF).reshape(cells, FRAMES, COUT)
        k_ref[src] = key.astype(BF).reshape(cells, FRAMES, COUT)
        v_ref[src] = mapped[:, 2 * COUT :].astype(BF).reshape(cells, FRAMES, COUT)
        return carry

    lax.fori_loop(0, ctx, project, 0)

    low = iota((1, 128), 1) < 64
    ones = [jnp.where(low, 1.0, 0.0), jnp.where(low, 0.0, 1.0)]
    block = min(128, total)

    def mix(cell, carry):
        for pair in range(2):
            lanes = slice(pair * 128, (pair + 1) * 128)
            key = k_ref[:, cell, :, lanes].reshape(total, 128)
            value = v_ref[:, cell, :, lanes].reshape(total, 128)
            zero = jnp.zeros_like(key)
            keys = jnp.concatenate([jnp.where(low, key, zero), jnp.where(low, zero, key)], axis=0)
            sides = [jnp.where(low, value, zero), jnp.where(low, zero, value)]
            flags = [jnp.broadcast_to(ones[n].astype(BF), (total, 128)) for n in range(2)]
            values = jnp.concatenate(
                [jnp.concatenate([sides[n], flags[n]], axis=1) for n in range(2)], axis=0
            )
            for at in range(0, total, block):
                part = slice(at // FRAMES, (at + block) // FRAMES)
                query = q_ref[part, cell, :, lanes].reshape(block, 128)
                logits = dot_t(query, keys)
                mask = bias[at : at + block, :]
                weights = jnp.exp(logits + jnp.concatenate([mask, mask], axis=1)).astype(BF)
                sums = dot(weights, values)
                mixed = (sums[:, :128] / sums[:, 128:]).astype(BF)
                q_ref[part, cell, :, lanes] = mixed.reshape(block // FRAMES, FRAMES, 128)
        return carry

    lax.fori_loop(0, cells, mix, 0)

    turn = swap_matrix(cells, FRAMES)

    for src in range(ctx):
        mixed = q_ref[src].reshape(main, COUT)
        value = rows_of[src].reshape(main, COUT).astype(F32)
        latent = (value + dot(mixed, last_ref[...])).astype(BF)
        out_refs[src // 2][src % 2] = dot(turn, latent).astype(BF)


def run_attend(assign, counts, scale, me, got, qkv, last, ctx):
    cells = ROWS * COLS // ctx
    total = ctx * FRAMES
    held = pltpu.VMEM((ctx, cells, FRAMES, COUT), BF)
    piece = (1, cells * (FRAMES + SLOTS), COUT)

    def whole(array):
        return pl.BlockSpec(array.shape, lambda i: (0,) * array.ndim)

    def half(n):
        return pl.BlockSpec(piece, lambda i: (n, 0, 0))

    out = (2, cells * FRAMES, COUT)
    return pl.pallas_call(
        functools.partial(attend_kernel, cells, ctx),
        grid=(1,),
        out_shape=[jax.ShapeDtypeStruct(out, BF)] * (ctx // 2),
        in_specs=[SMEM, SMEM, SMEM, SMEM, whole(qkv), whole(last)] + [half(n % 2) for n in range(ctx)],
        out_specs=[pl.BlockSpec(out, lambda i: (0, 0, 0))] * (ctx // 2),
        scratch_shapes=[
            pltpu.SMEM(assign.shape, jnp.int32),
            held,
            held,
            held,
            held,
            pltpu.VMEM((ctx, cells * SLOTS, COUT), BF),
            pltpu.VMEM((total, total), F32),
        ],
        compiler_params=params(),
        cost_estimate=cost(3_000_000_000, 4_000_000),
        name="attend",
    )(assign, counts, scale, me, qkv, last, *got)


def place_kernel(me_ref, *refs):
    out_ref = refs[-1]
    for n, ref in enumerate(refs[:-1]):
        out_ref[:, me_ref[0] ^ n] = ref[0]


def run_place(me, pieces, ctx):
    cells = ROWS * COLS // ctx
    pieces = [piece.reshape(2, FRAMES, cells, COUT) for piece in pieces]
    shape = (FRAMES, ctx, cells, COUT)

    def half(n):
        return pl.BlockSpec((1,) + pieces[0].shape[1:], lambda i: (n, 0, 0, 0))

    return pl.pallas_call(
        place_kernel,
        grid=(1,),
        out_shape=jax.ShapeDtypeStruct(shape, BF),
        in_specs=[SMEM] + [half(n % 2) for n in range(ctx)],
        out_specs=pl.BlockSpec(shape, lambda i: (0, 0, 0, 0)),
        compiler_params=params(),
        cost_estimate=cost(0, 2_000_000),
        name="place_latents",
    )(me, *pieces)


def flip(value, axis, size, bits):
    return lax.ppermute(value, axis, [(i, i ^ bits) for i in range(size)])


def exchange(parts, ctx, after=None):
    far = [parts[0]] + [None] * (len(parts) - 1)
    for k in reversed(range(1, len(parts))):
        far[k] = flip(parts[k], "ctx", ctx, 2 * k)
    if after is not None:
        far = lax.optimization_barrier((far, after))[0]
    near = [flip(part, "ctx", ctx, 1) for part in far]
    return [piece for pair in zip(far, near) for piece in pair]


def per_device(ctx, dp, frames, assign, counts, scale, taps, qkv, last, upstream):
    me = lax.axis_index("ctx").astype(jnp.int32).reshape(1)
    frames, upstream = frames[0], upstream[0]
    cells = ROWS * COLS // ctx
    chips = ctx // 2
    sent = run_conv(me, frames, taps, ctx)
    tails = exchange([run_tails(frames)] * chips, ctx, sent[0])
    got = exchange(sent, ctx)

    parts = run_grad(assign, counts, me, frames, upstream, sent[0], tails, ctx)
    sums = [kept + flip(part, "ctx", ctx, 1).astype(F32) for part, kept in zip(parts[:chips], parts[chips:])]
    share = sums[0]
    for k in reversed(range(1, chips)):
        share = share + flip(sums[k].astype(BF), "ctx", ctx, 2 * k).astype(F32)
    bits = 1
    while bits < dp:
        share = share.astype(BF)
        share = share.astype(F32) + flip(share, "dp", dp, bits).astype(F32)
        bits *= 2

    blended = run_attend(assign, counts, scale, me, got, qkv, last, ctx)
    latents = run_place(me, exchange(blended, ctx), ctx)
    return (latents.reshape(1, SLOTS, STEPS, ctx * cells, COUT), share)


def solution(mesh):
    placed = (
        P("dp", "ctx", None, None, None, None),
        P(),
        P(),
        P(),
        P(),
        P(),
        P(),
        P("dp", "ctx", None, None, None),
    )
    return jax.shard_map(
        functools.partial(per_device, mesh.shape["ctx"], mesh.shape["dp"]),
        mesh=mesh,
        in_specs=placed,
        out_specs=(P("dp", "ctx", None, None, None), P("ctx", None)),
        check_vma=False,
    )
```

```python
import functools

import jax
import jax.numpy as jnp
from jax import lax
from jax.experimental import pallas as pl
from jax.experimental.pallas import tpu as pltpu
from jax.sharding import PartitionSpec as P

BF = jnp.bfloat16
F32 = jnp.float32
MIB = 1024 * 1024
ROWS, COLS, CIN, COUT = 8, 16, 128, 256
SLOTS, STEPS = 4, 4
FRAMES = SLOTS * STEPS
PADDED = (3, ROWS + 2, COLS + 2, FRAMES, CIN)
TAPS = [(h, w) for h in range(3) for w in range(3)]
TAP_SETS = [TAPS[0:2], TAPS[2:4], TAPS[4:6], TAPS[6:8], TAPS[8:9]]


def iota(shape, axis):
    return lax.broadcasted_iota(jnp.int32, shape, axis)


def dot(a, b):
    return jnp.dot(a, b, preferred_element_type=F32)


def dot_t(a, b):
    return lax.dot_general(a, b, (((1,), (1,)), ((), ())), preferred_element_type=F32)


def swap_matrix(outer, inner):
    total = outer * inner
    i, j = iota((total, total), 0), iota((total, total), 1)
    return ((i % outer == j // inner) & (i // outer == j % inner)).astype(F32).astype(BF)


def params(mib):
    return pltpu.CompilerParams(vmem_limit_bytes=mib * MIB)


def cost(flops, nbytes):
    return pl.CostEstimate(flops=flops, bytes_accessed=nbytes, transcendentals=0)


VMEM = pl.BlockSpec(memory_space=pltpu.VMEM)
SMEM = pl.BlockSpec(memory_space=pltpu.SMEM)
HBM = pl.BlockSpec(memory_space=pltpu.HBM)
ANY = pl.BlockSpec(memory_space=pl.ANY)


def fill_slots(assign, slot_of):
    def body(i, carry):
        slot_of[assign[i]] = i
        return carry

    lax.fori_loop(0, assign.shape[0], body, 0)


def is_opening(span, counts):
    start, found = jnp.int32(0), jnp.int32(0)
    for k in range(counts.shape[0]):
        found = jnp.where(span == start, jnp.int32(1), found)
        start = start + counts[k]
    return found


def lay_out_taps(x_ref, prev, padded):
    padded[...] = jnp.zeros_like(padded)
    swap = swap_matrix(FRAMES, COLS)

    def tile(s, f, r):
        return x_ref[s, f, r] if f >= 0 else prev(s, f, r)

    for r in range(0, ROWS, 2):
        for kt in range(3):
            cols = [
                jnp.concatenate([tile(s, 2 * t - 2 + kt, rr) for s in range(SLOTS) for t in range(STEPS)], axis=0)
                for rr in (r, r + 1)
            ]
            turned = dot(swap, jnp.concatenate(cols, axis=1)).astype(BF)
            for n in range(2):
                part = turned[:, n * CIN : (n + 1) * CIN].reshape(COLS, FRAMES, CIN)
                padded[kt, r + n + 1, 1 : COLS + 1] = part


def tap_block(padded, taps):
    blocks = [
        padded[kt, h : h + ROWS, w : w + COLS].reshape(ROWS * COLS * FRAMES, CIN) for h, w in taps for kt in range(3)
    ]
    return jnp.concatenate(blocks, axis=1)


def tap_rows(kt, h, w):
    at = ((kt * 3 + h) * 3 + w) * CIN
    return slice(at, at + CIN)


def device_at(me, chip_bits, core_bit):
    return me ^ (2 * chip_bits + core_bit)


def conv_kernel(cells, me_ref, x_ref, w_ref, *refs):
    out_refs, (main_part, edge_part, padded, edge, x_in, w_in, sem) = refs[:-7], refs[-7:]
    copies = [pltpu.make_async_copy(x_ref, x_in, sem.at[0]), pltpu.make_async_copy(w_ref, w_in, sem.at[1])]
    for copy in copies:
        copy.start()
    x_ref, w_ref = x_in, w_in
    copies[0].wait()
    lay_out_taps(x_ref, lambda s, f, r: jnp.zeros((COLS, CIN), BF), padded)
    wide = SLOTS * COLS
    i, j = iota((3 * wide, wide), 0), iota((3 * wide, wide), 1)
    k = i % wide
    q = (k // (SLOTS * cells)) * cells + k % cells
    s = (k // cells) % SLOTS
    shift = ((j // COLS == s) & (j % COLS == q + i // wide - 1)).astype(F32).astype(BF)
    edge[0] = jnp.zeros_like(edge[0])
    edge[ROWS + 1] = jnp.zeros_like(edge[0])
    for r in range(ROWS):
        tails = jnp.concatenate(
            [jnp.concatenate([x_ref[s, f, r] for s in range(SLOTS)], axis=0) for f in (6, 7)], axis=1
        )
        edge[r + 1] = dot(shift, tails).astype(BF)
    copies[1].wait()
    total = None
    for taps in TAP_SETS:
        rows = jnp.concatenate([w_ref[tap_rows(kt, h, w), :] for h, w in taps for kt in range(3)], axis=0)
        term = dot(tap_block(padded, taps), rows)
        total = term if total is None else total + term
    main = cells * FRAMES
    main_part[...] = total.astype(BF).reshape(main_part.shape)
    carry = None
    for h, w in TAPS:
        rows = jnp.concatenate([w_ref[tap_rows(kt, h, w), :] for kt in range(2)], axis=0)
        part = edge[h : h + ROWS, w * wide : (w + 1) * wide, :].reshape(ROWS * wide, 2 * CIN)
        term = dot(part, rows)
        carry = term if carry is None else carry + term
    edge_part[...] = carry.astype(BF).reshape(edge_part.shape)
    me = me_ref[0]
    for k, ref in enumerate(out_refs):
        for c in range(2):
            to = device_at(me, k, c)
            ref[c, :main, :] = main_part[to]
            ref[c, main:, :] = edge_part[to]


def run_conv(me, frames, taps, ctx):
    cells = ROWS * COLS // ctx
    return pl.pallas_call(
        functools.partial(conv_kernel, cells),
        out_shape=[jax.ShapeDtypeStruct((2, cells * (FRAMES + SLOTS), COUT), BF)] * (ctx // 2),
        in_specs=[SMEM, HBM, HBM],
        out_specs=[VMEM] * (ctx // 2),
        scratch_shapes=[
            pltpu.VMEM((ctx, cells * FRAMES, COUT), BF),
            pltpu.VMEM((ctx, cells * SLOTS, COUT), BF),
            pltpu.VMEM(PADDED, BF),
            pltpu.VMEM((ROWS + 2, 3 * SLOTS * COLS, 2 * CIN), BF),
            pltpu.VMEM(frames.shape, BF),
            pltpu.VMEM(taps.shape, BF),
            pltpu.SemaphoreType.DMA((2,)),
        ],
        compiler_params=params(24),
        cost_estimate=cost(4_800_000_000, 4_000_000),
        name="conv_forward",
    )(me, frames, taps)


def tails_kernel(x_ref, out_ref, sem):
    copy = pltpu.make_async_copy(x_ref.at[:, 6:8], out_ref, sem)
    copy.start()
    copy.wait()


def run_tails(frames):
    return pl.pallas_call(
        tails_kernel,
        out_shape=jax.ShapeDtypeStruct((SLOTS, 2, ROWS, COLS, CIN), BF),
        in_specs=[HBM],
        out_specs=VMEM,
        scratch_shapes=[pltpu.SemaphoreType.DMA],
        compiler_params=params(4),
        cost_estimate=cost(0, 500_000),
        name="cut_tails",
    )(frames)


def grad_kernel(chips, assign, counts, me_ref, xs_ref, xo_ref, us_ref, uo_ref, *refs):
    tails, refs = refs[: 2 * chips], refs[2 * chips :]
    out_refs = refs[:chips]
    slot_of, padded, turned, product, before, sem = refs[chips:]
    fill_slots(assign, slot_of)
    me = me_ref[0]
    openings = []
    for core in range(2):
        for i in range(SLOTS):
            span = assign[(me ^ core) * SLOTS + i]
            openings.append(is_opening(span, counts))
            slot = slot_of[jnp.maximum(span - 1, 0)]
            apart = (slot // SLOTS) ^ me
            for n, ref in enumerate(tails):

                @pl.when(apart == n)
                def _():
                    at = core * SLOTS + i
                    pltpu.make_async_copy(ref.at[slot % SLOTS], before.at[at], sem.at[at]).start()

    for at in range(2 * SLOTS):
        pltpu.make_async_copy(tails[0].at[0], before.at[at], sem.at[at]).wait()

    swap = swap_matrix(FRAMES, COLS)
    span_rows = COLS * FRAMES
    total = ROWS * span_rows
    for core, (x_ref, u_ref) in enumerate(((xs_ref, us_ref), (xo_ref, uo_ref))):

        def prev(s, f, r):
            got = before[core * SLOTS + s, f + 2, r]
            return jnp.where(openings[core * SLOTS + s] > 0, jnp.zeros_like(got), got)

        lay_out_taps(x_ref, prev, padded.at[core])
        for r in range(ROWS):
            block = jnp.concatenate(
                [u_ref[s, t, r * COLS : (r + 1) * COLS, :] for s in range(SLOTS) for t in range(STEPS)], axis=0
            )
            at = core * total + r * span_rows
            turned[:, at : at + span_rows] = dot(swap, block).T.astype(BF)

    def entries(tap):
        kt, h, w = tap // 9, (tap // 3) % 3, tap % 3
        cores = [
            padded[core, kt, pl.ds(h, ROWS), pl.ds(w, COLS)].reshape(total, CIN) for core in range(2)
        ]
        return jnp.concatenate(cores, axis=0)

    rows = out_refs[0].shape[0]
    count = -(-rows // CIN)
    for k, ref in enumerate(out_refs):
        first = device_at(me, k, 0) * rows
        tap, offset = first // CIN, first % CIN
        near = jnp.concatenate([entries(jnp.minimum(tap + n, 26)) for n in range(count)], axis=1)
        product[: count * CIN, :] = dot(turned[...], near).T

        @pl.when(offset + rows > count * CIN)
        def _():
            product[count * CIN :, :] = dot(turned[...], entries(jnp.minimum(tap + count, 26))).T

        if rows % 16 == 0:
            ref[...] = product[pl.ds(pl.multiple_of(offset, 16), rows), :].astype(ref.dtype)
        else:
            size = product.shape[0]
            ref[...] = pltpu.roll(product[...], (size - offset) % size, 0)[:rows].astype(ref.dtype)


def run_grad(assign, counts, me, frames, upstream, tails, ctx):
    chips, rows = ctx // 2, 27 * CIN // ctx
    return pl.pallas_call(
        functools.partial(grad_kernel, chips),
        out_shape=[jax.ShapeDtypeStruct((rows, COUT), F32 if k == 0 else BF) for k in range(chips)],
        in_specs=[SMEM, SMEM, SMEM, VMEM, VMEM, VMEM, VMEM] + [ANY] * ctx,
        out_specs=[VMEM] * chips,
        scratch_shapes=[
            pltpu.SMEM(assign.shape, jnp.int32),
            pltpu.VMEM((2,) + PADDED, BF),
            pltpu.VMEM((COUT, 2 * ROWS * COLS * FRAMES), BF),
            pltpu.VMEM(((-(-rows // CIN) + 1) * CIN, COUT), F32),
            pltpu.VMEM((2 * SLOTS, 2, ROWS, COLS, CIN), BF),
            pltpu.SemaphoreType.DMA((2 * SLOTS,)),
        ],
        compiler_params=params(32),
        cost_estimate=cost(1000, 1000),
        name="conv_gradient",
    )(assign, counts, me, *frames, *upstream, *tails)


def attend_kernel(cells, ctx, assign, counts, scale, me_ref, qkv_ref, last_ref, *refs):
    chips = ctx // 2
    got_refs, out_refs = refs[:ctx], refs[ctx : ctx + chips]
    slot_of, rows_of, q_ref, k_ref, v_ref, edges, bias = refs[ctx + chips :]
    me = me_ref[0]
    main = cells * FRAMES
    total = ctx * FRAMES
    fill_slots(assign, slot_of)

    def mark(shape, axis):
        spot = iota(shape, axis)
        span = jnp.zeros(shape, jnp.int32)
        for i in range(ctx * SLOTS):
            span = jnp.where(spot // STEPS == i, assign[(me ^ (i // SLOTS)) * SLOTS + i % SLOTS], span)
        clip, end = jnp.zeros(shape, jnp.int32), jnp.int32(0)
        for k in range(counts.shape[0]):
            end = end + counts[k]
            clip = clip + (span >= end).astype(jnp.int32)
        return span * STEPS + spot % STEPS, clip

    time_b, clip_b = mark((1, total), 1)
    time_a, clip_a = mark((total, 1), 0)
    allowed = (clip_a == clip_b) & (time_b <= time_a)
    bias[...] = jnp.where(allowed, 0.0, -1e30)

    i, j = iota((main, main), 0), iota((main, main), 1)
    held = j // (SLOTS * cells)
    fits = (i % STEPS == 0) & ((i // STEPS) % SLOTS == held) & (i // FRAMES == j % cells)
    base = jnp.where(fits, 1, 0)
    lane = iota((1, main), 1)
    from_slot = (lane // cells) % SLOTS
    lane_held = lane // (SLOTS * cells)
    same_head = (iota((COUT, COUT), 0) // 64 == iota((COUT, COUT), 1) // 64).astype(F32).astype(BF)
    head = iota((1, COUT), 1) // 64
    gain = jnp.zeros((1, COUT), F32)
    for h in range(COUT // 64):
        gain = jnp.where(head == h, scale[h], gain)

    for src in range(ctx):
        edges[src] = got_refs[src][0, main:, :]
        rows_of[src] = got_refs[src][0, :main, :].reshape(cells, FRAMES, COUT)

    def project(src, carry):
        pick = jnp.full((1, main), -1, jnp.int32)
        blocks = []
        for s in range(SLOTS):
            span = assign[(me ^ src) * SLOTS + s]
            slot = slot_of[jnp.maximum(span - 1, 0)]
            spot = jnp.where(is_opening(span, counts) > 0, -1, slot % SLOTS)
            pick = jnp.where(lane_held == s, spot, pick)
            blocks.append(edges[(slot // SLOTS) ^ me])
        chosen = jnp.where(pick == from_slot, base, 0).astype(F32).astype(BF)
        value = rows_of[src].reshape(main, COUT).astype(F32) + dot(chosen, jnp.concatenate(blocks, axis=0))
        value = value.astype(BF)
        rows_of[src] = value.reshape(cells, FRAMES, COUT)
        value = value.astype(F32)
        normed = value * lax.rsqrt(jnp.mean(value * value, axis=-1, keepdims=True) + 1e-6)
        mapped = dot(normed.astype(BF), qkv_ref[...])
        query, key = mapped[:, :COUT], mapped[:, COUT : 2 * COUT]
        query = query * (lax.rsqrt(dot((query * query).astype(BF), same_head) + 1e-6) * gain)
        key = key * lax.rsqrt(dot((key * key).astype(BF), same_head) + 1e-6)
        q_ref[src] = query.astype(BF).reshape(cells, FRAMES, COUT)
        k_ref[src] = key.astype(BF).reshape(cells, FRAMES, COUT)
        v_ref[src] = mapped[:, 2 * COUT :].astype(BF).reshape(cells, FRAMES, COUT)
        return carry

    lax.fori_loop(0, ctx, project, 0)

    low = iota((1, 128), 1) < 64
    ones = [jnp.where(low, 1.0, 0.0), jnp.where(low, 0.0, 1.0)]
    block = min(128, total)

    def mix(cell, carry):
        for pair in range(2):
            lanes = slice(pair * 128, (pair + 1) * 128)
            key = k_ref[:, cell, :, lanes].reshape(total, 128)
            value = v_ref[:, cell, :, lanes].reshape(total, 128)
            zero = jnp.zeros_like(key)
            keys = jnp.concatenate([jnp.where(low, key, zero), jnp.where(low, zero, key)], axis=0)
            sides = [jnp.where(low, value, zero), jnp.where(low, zero, value)]
            flags = [jnp.broadcast_to(ones[n].astype(BF), (total, 128)) for n in range(2)]
            values = jnp.concatenate(
                [jnp.concatenate([sides[n], flags[n]], axis=1) for n in range(2)], axis=0
            )
            for at in range(0, total, block):
                part = slice(at // FRAMES, (at + block) // FRAMES)
                query = q_ref[part, cell, :, lanes].reshape(block, 128)
                logits = dot_t(query, keys)
                mask = bias[at : at + block, :]
                weights = jnp.exp(logits + jnp.concatenate([mask, mask], axis=1)).astype(BF)
                sums = dot(weights, values)
                mixed = (sums[:, :128] / sums[:, 128:]).astype(BF)
                q_ref[part, cell, :, lanes] = mixed.reshape(block // FRAMES, FRAMES, 128)
        return carry

    lax.fori_loop(0, cells, mix, 0)

    turn = swap_matrix(cells, FRAMES)

    for src in range(ctx):
        mixed = q_ref[src].reshape(main, COUT)
        value = rows_of[src].reshape(main, COUT).astype(F32)
        latent = (value + dot(mixed, last_ref[...])).astype(BF)
        out_refs[src // 2][src % 2] = dot(turn, latent).astype(BF)


def run_attend(assign, counts, scale, me, got, qkv, last, ctx):
    cells = ROWS * COLS // ctx
    total = ctx * FRAMES
    held = pltpu.VMEM((ctx, cells, FRAMES, COUT), BF)
    piece = (1, cells * (FRAMES + SLOTS), COUT)

    def whole(array):
        return pl.BlockSpec(array.shape, lambda i: (0,) * array.ndim)

    def half(n):
        return pl.BlockSpec(piece, lambda i: (n, 0, 0))

    out = (2, cells * FRAMES, COUT)
    return pl.pallas_call(
        functools.partial(attend_kernel, cells, ctx),
        grid=(1,),
        out_shape=[jax.ShapeDtypeStruct(out, BF)] * (ctx // 2),
        in_specs=[SMEM, SMEM, SMEM, SMEM, whole(qkv), whole(last)] + [half(n % 2) for n in range(ctx)],
        out_specs=[pl.BlockSpec(out, lambda i: (0, 0, 0))] * (ctx // 2),
        scratch_shapes=[
            pltpu.SMEM(assign.shape, jnp.int32),
            held,
            held,
            held,
            held,
            pltpu.VMEM((ctx, cells * SLOTS, COUT), BF),
            pltpu.VMEM((total, total), F32),
        ],
        compiler_params=params(24),
        cost_estimate=cost(3_000_000_000, 4_000_000),
        name="attend",
    )(assign, counts, scale, me, qkv, last, *got)


def place_kernel(me_ref, *refs):
    out_ref = refs[-1]
    for n, ref in enumerate(refs[:-1]):
        out_ref[:, me_ref[0] ^ n] = ref[0]


def run_place(me, pieces, ctx):
    cells = ROWS * COLS // ctx
    pieces = [piece.reshape(2, FRAMES, cells, COUT) for piece in pieces]
    shape = (FRAMES, ctx, cells, COUT)

    def half(n):
        return pl.BlockSpec((1,) + pieces[0].shape[1:], lambda i: (n, 0, 0, 0))

    return pl.pallas_call(
        place_kernel,
        grid=(1,),
        out_shape=jax.ShapeDtypeStruct(shape, BF),
        in_specs=[SMEM] + [half(n % 2) for n in range(ctx)],
        out_specs=pl.BlockSpec(shape, lambda i: (0, 0, 0, 0)),
        compiler_params=params(8),
        cost_estimate=cost(0, 2_000_000),
        name="place_latents",
    )(me, *pieces)


def flip(value, axis, size, bits):
    return lax.ppermute(value, axis, [(i, i ^ bits) for i in range(size)])


def send_far(parts, ctx):
    far = [parts[0]] + [None] * (len(parts) - 1)
    for k in reversed(range(1, len(parts))):
        far[k] = flip(parts[k], "ctx", ctx, 2 * k)
    return far


def send_near(value, ctx):
    return flip(value, "ctx", ctx, 1)


def hold(values, after):
    return lax.optimization_barrier((values, after))[0]


def weave(far, near):
    return [piece for pair in zip(far, near) for piece in pair]


def per_device(ctx, dp, frames, assign, counts, scale, taps, qkv, last, upstream):
    me = lax.axis_index("ctx").astype(jnp.int32).reshape(1)
    frames, upstream = frames[0], upstream[0]
    cells = ROWS * COLS // ctx
    chips = ctx // 2
    both_frames = (frames, send_near(frames, ctx))
    both_upstream = (upstream, send_near(upstream, ctx))
    tails = send_far([run_tails(frames)] * chips, ctx)
    sent = run_conv(me, frames, taps, ctx)
    got = send_far(sent, ctx)

    tails = hold(tails, sent[0])
    tails = weave(tails, [send_near(part, ctx) for part in tails])
    halves = run_grad(assign, counts, me, both_frames, both_upstream, tails, ctx)
    got = [got[0]] + hold(got[1:], halves[1:])
    got_near = [send_near(part, ctx) for part in got]
    moved = [flip(halves[k], "ctx", ctx, 2 * k) for k in range(1, chips)]
    blended = run_attend(assign, counts, scale, me, weave(got, got_near), qkv, last, ctx)
    share = halves[0]
    for part in hold(moved, blended[0]):
        share = share + part.astype(F32)
    back = send_far(blended, ctx)
    bits = 1
    while bits < dp:
        share = share.astype(BF)
        share = share.astype(F32) + flip(share, "dp", dp, bits).astype(F32)
        bits *= 2
    latents = run_place(me, weave(back, [send_near(part, ctx) for part in back]), ctx)
    return (latents.reshape(1, SLOTS, STEPS, ctx * cells, COUT), share)


def solution(mesh):
    placed = (
        P("dp", "ctx", None, None, None, None),
        P(),
        P(),
        P(),
        P(),
        P(),
        P(),
        P("dp", "ctx", None, None, None),
    )
    return jax.shard_map(
        functools.partial(per_device, mesh.shape["ctx"], mesh.shape["dp"]),
        mesh=mesh,
        in_specs=placed,
        out_specs=(P("dp", "ctx", None, None, None), P("ctx", None)),
        check_vma=False,
    )
```

```python
import functools

import jax
import jax.numpy as jnp
from jax import lax
from jax.experimental import pallas as pl
from jax.experimental.pallas import tpu as pltpu
from jax.sharding import PartitionSpec as P

BF = jnp.bfloat16
F32 = jnp.float32
MIB = 1024 * 1024
ROWS, COLS, CIN, COUT = 8, 16, 128, 256
SLOTS, STEPS = 4, 4
FRAMES = SLOTS * STEPS
PADDED = (3, ROWS + 2, COLS + 2, FRAMES, CIN)
TAPS = [(h, w) for h in range(3) for w in range(3)]
TAP_SETS = [TAPS[0:2], TAPS[2:4], TAPS[4:6], TAPS[6:8], TAPS[8:9]]


def iota(shape, axis):
    return lax.broadcasted_iota(jnp.int32, shape, axis)


def dot(a, b):
    return jnp.dot(a, b, preferred_element_type=F32)


def dot_t(a, b):
    return lax.dot_general(a, b, (((1,), (1,)), ((), ())), preferred_element_type=F32)


def swap_matrix(outer, inner):
    total = outer * inner
    i, j = iota((total, total), 0), iota((total, total), 1)
    return ((i % outer == j // inner) & (i // outer == j % inner)).astype(F32).astype(BF)


def params(mib):
    return pltpu.CompilerParams(vmem_limit_bytes=mib * MIB)


def cost(flops, nbytes):
    return pl.CostEstimate(flops=flops, bytes_accessed=nbytes, transcendentals=0)


VMEM = pl.BlockSpec(memory_space=pltpu.VMEM)
SMEM = pl.BlockSpec(memory_space=pltpu.SMEM)
HBM = pl.BlockSpec(memory_space=pltpu.HBM)
ANY = pl.BlockSpec(memory_space=pl.ANY)


def fill_slots(assign, slot_of):
    def body(i, carry):
        slot_of[assign[i]] = i
        return carry

    lax.fori_loop(0, assign.shape[0], body, 0)


def is_opening(span, counts):
    start, found = jnp.int32(0), jnp.int32(0)
    for k in range(counts.shape[0]):
        found = jnp.where(span == start, jnp.int32(1), found)
        start = start + counts[k]
    return found


def lay_out_taps(x_ref, prev, padded):
    padded[...] = jnp.zeros_like(padded)
    swap = swap_matrix(FRAMES, COLS)

    def tile(s, f, r):
        return x_ref[s, f, r] if f >= 0 else prev(s, f, r)

    for r in range(0, ROWS, 2):
        for kt in range(3):
            cols = [
                jnp.concatenate([tile(s, 2 * t - 2 + kt, rr) for s in range(SLOTS) for t in range(STEPS)], axis=0)
                for rr in (r, r + 1)
            ]
            turned = dot(swap, jnp.concatenate(cols, axis=1)).astype(BF)
            for n in range(2):
                part = turned[:, n * CIN : (n + 1) * CIN].reshape(COLS, FRAMES, CIN)
                padded[kt, r + n + 1, 1 : COLS + 1] = part


def tap_block(padded, taps):
    blocks = [
        padded[kt, h : h + ROWS, w : w + COLS].reshape(ROWS * COLS * FRAMES, CIN) for h, w in taps for kt in range(3)
    ]
    return jnp.concatenate(blocks, axis=1)


def tap_rows(kt, h, w):
    at = ((kt * 3 + h) * 3 + w) * CIN
    return slice(at, at + CIN)


def device_at(me, chip_bits, core_bit):
    return me ^ (2 * chip_bits + core_bit)


def conv_kernel(cells, me_ref, x_ref, w_ref, *refs):
    out_refs, (main_part, edge_part, padded, edge, x_in, w_in, sem) = refs[:-7], refs[-7:]
    copies = [pltpu.make_async_copy(x_ref, x_in, sem.at[0]), pltpu.make_async_copy(w_ref, w_in, sem.at[1])]
    for copy in copies:
        copy.start()
    x_ref, w_ref = x_in, w_in
    copies[0].wait()
    lay_out_taps(x_ref, lambda s, f, r: jnp.zeros((COLS, CIN), BF), padded)
    wide = SLOTS * COLS
    i, j = iota((3 * wide, wide), 0), iota((3 * wide, wide), 1)
    k = i % wide
    q = (k // (SLOTS * cells)) * cells + k % cells
    s = (k // cells) % SLOTS
    shift = ((j // COLS == s) & (j % COLS == q + i // wide - 1)).astype(F32).astype(BF)
    edge[0] = jnp.zeros_like(edge[0])
    edge[ROWS + 1] = jnp.zeros_like(edge[0])
    for r in range(ROWS):
        tails = jnp.concatenate(
            [jnp.concatenate([x_ref[s, f, r] for s in range(SLOTS)], axis=0) for f in (6, 7)], axis=1
        )
        edge[r + 1] = dot(shift, tails).astype(BF)
    copies[1].wait()
    total = None
    for taps in TAP_SETS:
        rows = jnp.concatenate([w_ref[tap_rows(kt, h, w), :] for h, w in taps for kt in range(3)], axis=0)
        term = dot(tap_block(padded, taps), rows)
        total = term if total is None else total + term
    main = cells * FRAMES
    main_part[...] = total.astype(BF).reshape(main_part.shape)
    carry = None
    for h, w in TAPS:
        rows = jnp.concatenate([w_ref[tap_rows(kt, h, w), :] for kt in range(2)], axis=0)
        part = edge[h : h + ROWS, w * wide : (w + 1) * wide, :].reshape(ROWS * wide, 2 * CIN)
        term = dot(part, rows)
        carry = term if carry is None else carry + term
    edge_part[...] = carry.astype(BF).reshape(edge_part.shape)
    me = me_ref[0]
    for k, ref in enumerate(out_refs):
        for c in range(2):
            to = device_at(me, k, c)
            ref[c, :main, :] = main_part[to]
            ref[c, main:, :] = edge_part[to]


def run_conv(me, frames, taps, ctx):
    cells = ROWS * COLS // ctx
    return pl.pallas_call(
        functools.partial(conv_kernel, cells),
        out_shape=[jax.ShapeDtypeStruct((2, cells * (FRAMES + SLOTS), COUT), BF)] * (ctx // 2),
        in_specs=[SMEM, HBM, HBM],
        out_specs=[VMEM] * (ctx // 2),
        scratch_shapes=[
            pltpu.VMEM((ctx, cells * FRAMES, COUT), BF),
            pltpu.VMEM((ctx, cells * SLOTS, COUT), BF),
            pltpu.VMEM(PADDED, BF),
            pltpu.VMEM((ROWS + 2, 3 * SLOTS * COLS, 2 * CIN), BF),
            pltpu.VMEM(frames.shape, BF),
            pltpu.VMEM(taps.shape, BF),
            pltpu.SemaphoreType.DMA((2,)),
        ],
        compiler_params=params(50),
        cost_estimate=cost(4_800_000_000, 4_000_000),
        name="conv_forward",
    )(me, frames, taps)


def tails_kernel(x_ref, out_ref, sem):
    copy = pltpu.make_async_copy(x_ref.at[:, 6:8], out_ref, sem)
    copy.start()
    copy.wait()


def run_tails(frames):
    return pl.pallas_call(
        tails_kernel,
        out_shape=jax.ShapeDtypeStruct((SLOTS, 2, ROWS, COLS, CIN), BF),
        in_specs=[HBM],
        out_specs=VMEM,
        scratch_shapes=[pltpu.SemaphoreType.DMA],
        compiler_params=params(4),
        cost_estimate=cost(0, 500_000),
        name="cut_tails",
    )(frames)


def grad_kernel(chips, assign, counts, me_ref, xs_ref, xo_ref, us_ref, uo_ref, *refs):
    tails, refs = refs[: 2 * chips], refs[2 * chips :]
    out_refs = refs[:chips]
    slot_of, padded, turned, product, before, sem = refs[chips:]
    fill_slots(assign, slot_of)
    me = me_ref[0]
    openings = []
    for core in range(2):
        for i in range(SLOTS):
            span = assign[(me ^ core) * SLOTS + i]
            openings.append(is_opening(span, counts))
            slot = slot_of[jnp.maximum(span - 1, 0)]
            apart = (slot // SLOTS) ^ me
            for n, ref in enumerate(tails):

                @pl.when(apart == n)
                def _():
                    at = core * SLOTS + i
                    pltpu.make_async_copy(ref.at[slot % SLOTS], before.at[at], sem.at[at]).start()

    for at in range(2 * SLOTS):
        pltpu.make_async_copy(tails[0].at[0], before.at[at], sem.at[at]).wait()

    swap = swap_matrix(FRAMES, COLS)
    span_rows = COLS * FRAMES
    total = ROWS * span_rows
    for core, (x_ref, u_ref) in enumerate(((xs_ref, us_ref), (xo_ref, uo_ref))):

        def prev(s, f, r):
            got = before[core * SLOTS + s, f + 2, r]
            return jnp.where(openings[core * SLOTS + s] > 0, jnp.zeros_like(got), got)

        lay_out_taps(x_ref, prev, padded.at[core])
        for r in range(ROWS):
            block = jnp.concatenate(
                [u_ref[s, t, r * COLS : (r + 1) * COLS, :] for s in range(SLOTS) for t in range(STEPS)], axis=0
            )
            at = core * total + r * span_rows
            turned[:, at : at + span_rows] = dot(swap, block).T.astype(BF)

    def entries(tap):
        kt, h, w = tap // 9, (tap // 3) % 3, tap % 3
        cores = [
            padded[core, kt, pl.ds(h, ROWS), pl.ds(w, COLS)].reshape(total, CIN) for core in range(2)
        ]
        return jnp.concatenate(cores, axis=0)

    rows = out_refs[0].shape[0]
    count = -(-rows // CIN)
    for k, ref in enumerate(out_refs):
        first = device_at(me, k, 0) * rows
        tap, offset = first // CIN, first % CIN
        near = jnp.concatenate([entries(jnp.minimum(tap + n, 26)) for n in range(count)], axis=1)
        product[: count * CIN, :] = dot(turned[...], near).T

        @pl.when(offset + rows > count * CIN)
        def _():
            product[count * CIN :, :] = dot(turned[...], entries(jnp.minimum(tap + count, 26))).T

        if rows % 16 == 0:
            ref[...] = product[pl.ds(pl.multiple_of(offset, 16), rows), :].astype(ref.dtype)
        else:
            size = product.shape[0]
            ref[...] = pltpu.roll(product[...], (size - offset) % size, 0)[:rows].astype(ref.dtype)


def run_grad(assign, counts, me, frames, upstream, tails, ctx):
    chips, rows = ctx // 2, 27 * CIN // ctx
    return pl.pallas_call(
        functools.partial(grad_kernel, chips),
        out_shape=[jax.ShapeDtypeStruct((rows, COUT), F32 if k == 0 else BF) for k in range(chips)],
        in_specs=[SMEM, SMEM, SMEM, VMEM, VMEM, VMEM, VMEM] + [ANY] * ctx,
        out_specs=[VMEM] * chips,
        scratch_shapes=[
            pltpu.SMEM(assign.shape, jnp.int32),
            pltpu.VMEM((2,) + PADDED, BF),
            pltpu.VMEM((COUT, 2 * ROWS * COLS * FRAMES), BF),
            pltpu.VMEM(((-(-rows // CIN) + 1) * CIN, COUT), F32),
            pltpu.VMEM((2 * SLOTS, 2, ROWS, COLS, CIN), BF),
            pltpu.SemaphoreType.DMA((2 * SLOTS,)),
        ],
        compiler_params=params(32),
        cost_estimate=cost(1000, 1000),
        name="conv_gradient",
    )(assign, counts, me, *frames, *upstream, *tails)


def attend_kernel(cells, ctx, assign, counts, scale, me_ref, qkv_ref, last_ref, *refs):
    chips = ctx // 2
    got_refs, out_refs = refs[:ctx], refs[ctx : ctx + chips]
    slot_of, rows_of, q_ref, k_ref, v_ref, edges, bias = refs[ctx + chips :]
    me = me_ref[0]
    main = cells * FRAMES
    total = ctx * FRAMES
    block = min(128, total)
    fill_slots(assign, slot_of)

    def mark(shape, axis):
        spot = iota(shape, axis)
        span = jnp.zeros(shape, jnp.int32)
        for i in range(ctx * SLOTS):
            span = jnp.where(spot // STEPS == i, assign[(me ^ (i // SLOTS)) * SLOTS + i % SLOTS], span)
        clip, end = jnp.zeros(shape, jnp.int32), jnp.int32(0)
        for k in range(counts.shape[0]):
            end = end + counts[k]
            clip = clip + (span >= end).astype(jnp.int32)
        return span * STEPS + spot % STEPS, clip

    time_b, clip_b = mark((1, total), 1)
    time_a, clip_a = mark((total, 1), 0)
    allowed = (clip_a == clip_b) & (time_b <= time_a)
    bias[...] = jnp.where(allowed, 0.0, -1e30)

    i, j = iota((main, main), 0), iota((main, main), 1)
    held = j // (SLOTS * cells)
    fits = (i % STEPS == 0) & ((i // STEPS) % SLOTS == held) & (i // FRAMES == j % cells)
    base = jnp.where(fits, 1, 0)
    lane = iota((1, main), 1)
    from_slot = (lane // cells) % SLOTS
    lane_held = lane // (SLOTS * cells)
    same_head = (iota((COUT, COUT), 0) // 64 == iota((COUT, COUT), 1) // 64).astype(F32).astype(BF)
    head = iota((1, COUT), 1) // 64
    gain = jnp.zeros((1, COUT), F32)
    for h in range(COUT // 64):
        gain = jnp.where(head == h, scale[h], gain)

    for src in range(ctx):
        edges[src] = got_refs[src][0, main:, :]
        rows_of[src] = got_refs[src][0, :main, :].reshape(cells, FRAMES, COUT)

    def project(src, carry):
        pick = jnp.full((1, main), -1, jnp.int32)
        blocks = []
        for s in range(SLOTS):
            span = assign[(me ^ src) * SLOTS + s]
            slot = slot_of[jnp.maximum(span - 1, 0)]
            spot = jnp.where(is_opening(span, counts) > 0, -1, slot % SLOTS)
            pick = jnp.where(lane_held == s, spot, pick)
            blocks.append(edges[(slot // SLOTS) ^ me])
        chosen = jnp.where(pick == from_slot, base, 0).astype(F32).astype(BF)
        value = rows_of[src].reshape(main, COUT).astype(F32) + dot(chosen, jnp.concatenate(blocks, axis=0))
        value = value.astype(BF)
        rows_of[src] = value.reshape(cells, FRAMES, COUT)
        value = value.astype(F32)
        normed = value * lax.rsqrt(jnp.mean(value * value, axis=-1, keepdims=True) + 1e-6)
        mapped = dot(normed.astype(BF), qkv_ref[...])
        query, key = mapped[:, :COUT], mapped[:, COUT : 2 * COUT]
        query = query * (lax.rsqrt(dot((query * query).astype(BF), same_head) + 1e-6) * gain)
        key = key * lax.rsqrt(dot((key * key).astype(BF), same_head) + 1e-6)
        q_ref[src] = query.astype(BF).reshape(cells, FRAMES, COUT)
        k_ref[src] = key.astype(BF).reshape(cells, FRAMES, COUT)
        v_ref[src] = mapped[:, 2 * COUT :].astype(BF).reshape(cells, FRAMES, COUT)
        return carry

    lax.fori_loop(0, ctx, project, 0, unroll=8 if total == block else 1)

    low = iota((1, 128), 1) < 64
    ones = [jnp.where(low, 1.0, 0.0), jnp.where(low, 0.0, 1.0)]

    def mix(cell, carry):
        for pair in range(2):
            lanes = slice(pair * 128, (pair + 1) * 128)
            key = k_ref[:, cell, :, lanes].reshape(total, 128)
            value = v_ref[:, cell, :, lanes].reshape(total, 128)
            zero = jnp.zeros_like(key)
            keys = jnp.concatenate([jnp.where(low, key, zero), jnp.where(low, zero, key)], axis=0)
            sides = [jnp.where(low, value, zero), jnp.where(low, zero, value)]
            flags = [jnp.broadcast_to(ones[n].astype(BF), (total, 128)) for n in range(2)]
            values = jnp.concatenate(
                [jnp.concatenate([sides[n], flags[n]], axis=1) for n in range(2)], axis=0
            )
            for at in range(0, total, block):
                part = slice(at // FRAMES, (at + block) // FRAMES)
                query = q_ref[part, cell, :, lanes].reshape(block, 128)
                logits = dot_t(query, keys)
                mask = bias[at : at + block, :]
                weights = jnp.exp(logits + jnp.concatenate([mask, mask], axis=1)).astype(BF)
                sums = dot(weights, values)
                mixed = (sums[:, :128] / sums[:, 128:]).astype(BF)
                q_ref[part, cell, :, lanes] = mixed.reshape(block // FRAMES, FRAMES, 128)
        return carry

    lax.fori_loop(0, cells, mix, 0, unroll=8 if total == block else 1)

    turn = swap_matrix(cells, FRAMES)

    for src in range(ctx):
        mixed = q_ref[src].reshape(main, COUT)
        value = rows_of[src].reshape(main, COUT).astype(F32)
        latent = (value + dot(mixed, last_ref[...])).astype(BF)
        out_refs[src // 2][src % 2] = dot(turn, latent).astype(BF)


def run_attend(assign, counts, scale, me, got, qkv, last, ctx):
    cells = ROWS * COLS // ctx
    total = ctx * FRAMES
    held = pltpu.VMEM((ctx, cells, FRAMES, COUT), BF)
    piece = (1, cells * (FRAMES + SLOTS), COUT)

    def whole(array):
        return pl.BlockSpec(array.shape, lambda i: (0,) * array.ndim)

    def half(n):
        return pl.BlockSpec(piece, lambda i: (n, 0, 0))

    out = (2, cells * FRAMES, COUT)
    return pl.pallas_call(
        functools.partial(attend_kernel, cells, ctx),
        grid=(1,),
        out_shape=[jax.ShapeDtypeStruct(out, BF)] * (ctx // 2),
        in_specs=[SMEM, SMEM, SMEM, SMEM, whole(qkv), whole(last)] + [half(n % 2) for n in range(ctx)],
        out_specs=[pl.BlockSpec(out, lambda i: (0, 0, 0))] * (ctx // 2),
        scratch_shapes=[
            pltpu.SMEM(assign.shape, jnp.int32),
            held,
            held,
            held,
            held,
            pltpu.VMEM((ctx, cells * SLOTS, COUT), BF),
            pltpu.VMEM((total, total), F32),
        ],
        compiler_params=params(24),
        cost_estimate=cost(1000, 1000),
        name="attend",
    )(assign, counts, scale, me, qkv, last, *got)


def place_kernel(me_ref, *refs):
    out_ref = refs[-1]
    for n, ref in enumerate(refs[:-1]):
        out_ref[:, me_ref[0] ^ n] = ref[0]


def run_place(me, pieces, ctx):
    cells = ROWS * COLS // ctx
    pieces = [piece.reshape(2, FRAMES, cells, COUT) for piece in pieces]
    shape = (FRAMES, ctx, cells, COUT)

    def half(n):
        return pl.BlockSpec((1,) + pieces[0].shape[1:], lambda i: (n, 0, 0, 0))

    return pl.pallas_call(
        place_kernel,
        grid=(1,),
        out_shape=jax.ShapeDtypeStruct(shape, BF),
        in_specs=[SMEM] + [half(n % 2) for n in range(ctx)],
        out_specs=pl.BlockSpec(shape, lambda i: (0, 0, 0, 0)),
        compiler_params=params(8),
        cost_estimate=cost(0, 2_000_000),
        name="place_latents",
    )(me, *pieces)


def flip(value, axis, size, bits):
    return lax.ppermute(value, axis, [(i, i ^ bits) for i in range(size)])


def send_far(parts, ctx):
    far = [parts[0]] + [None] * (len(parts) - 1)
    for k in reversed(range(1, len(parts))):
        far[k] = flip(parts[k], "ctx", ctx, 2 * k)
    return far


def send_near(value, ctx):
    return flip(value, "ctx", ctx, 1)


def hold(values, after):
    return lax.optimization_barrier((values, after))[0]


def weave(far, near):
    return [piece for pair in zip(far, near) for piece in pair]


def per_device(ctx, dp, frames, assign, counts, scale, taps, qkv, last, upstream):
    me = lax.axis_index("ctx").astype(jnp.int32).reshape(1)
    frames, upstream = frames[0], upstream[0]
    cells = ROWS * COLS // ctx
    chips = ctx // 2
    both_frames = (frames, send_near(frames, ctx))
    both_upstream = (upstream, send_near(upstream, ctx))
    tails = send_far([run_tails(frames)] * chips, ctx)
    sent = run_conv(me, frames, taps, ctx)
    got = send_far(sent, ctx)

    tails = hold(tails, sent[0])
    tails = weave(tails, [send_near(part, ctx) for part in tails])
    halves = run_grad(assign, counts, me, both_frames, both_upstream, tails, ctx)
    got = [got[0]] + hold(got[1:], halves[1:])
    got_near = [send_near(part, ctx) for part in got]
    moved = [flip(halves[k], "ctx", ctx, 2 * k) for k in range(1, chips)]
    blended = run_attend(assign, counts, scale, me, weave(got, got_near), qkv, last, ctx)
    share = halves[0]
    for part in hold(moved, blended[0]):
        share = share + part.astype(F32)
    back = send_far(blended, ctx)
    bits = 1
    while bits < dp:
        share = share.astype(BF)
        share = share.astype(F32) + flip(share, "dp", dp, bits).astype(F32)
        bits *= 2
    latents = run_place(me, weave(back, [send_near(part, ctx) for part in back]), ctx)
    return (latents.reshape(1, SLOTS, STEPS, ctx * cells, COUT), share)


def solution(mesh):
    placed = (
        P("dp", "ctx", None, None, None, None),
        P(),
        P(),
        P(),
        P(),
        P(),
        P(),
        P("dp", "ctx", None, None, None),
    )
    return jax.shard_map(
        functools.partial(per_device, mesh.shape["ctx"], mesh.shape["dp"]),
        mesh=mesh,
        in_specs=placed,
        out_specs=(P("dp", "ctx", None, None, None), P("ctx", None)),
        check_vma=False,
    )
```

```python
import functools

import jax
import jax.numpy as jnp
from jax import lax
from jax.experimental import pallas as pl
from jax.experimental.pallas import tpu as pltpu
from jax.sharding import PartitionSpec as P

BF = jnp.bfloat16
F32 = jnp.float32
MIB = 1024 * 1024
ROWS, COLS, CIN, COUT = 8, 16, 128, 256
SLOTS, STEPS = 4, 4
FRAMES = SLOTS * STEPS
PADDED = (3, ROWS + 2, COLS + 2, FRAMES, CIN)
TAPS = [(h, w) for h in range(3) for w in range(3)]
TAP_SETS = [TAPS[0:2], TAPS[2:4], TAPS[4:6], TAPS[6:8], TAPS[8:9]]


def iota(shape, axis):
    return lax.broadcasted_iota(jnp.int32, shape, axis)


def dot(a, b):
    return jnp.dot(a, b, preferred_element_type=F32)


def dot_t(a, b):
    return lax.dot_general(a, b, (((1,), (1,)), ((), ())), preferred_element_type=F32)


def swap_matrix(outer, inner):
    total = outer * inner
    i, j = iota((total, total), 0), iota((total, total), 1)
    return ((i % outer == j // inner) & (i // outer == j % inner)).astype(F32).astype(BF)


def params(mib):
    return pltpu.CompilerParams(vmem_limit_bytes=mib * MIB)


def cost(flops, nbytes):
    return pl.CostEstimate(flops=flops, bytes_accessed=nbytes, transcendentals=0)


VMEM = pl.BlockSpec(memory_space=pltpu.VMEM)
SMEM = pl.BlockSpec(memory_space=pltpu.SMEM)
HBM = pl.BlockSpec(memory_space=pltpu.HBM)
ANY = pl.BlockSpec(memory_space=pl.ANY)


def fill_slots(assign, slot_of):
    def body(i, carry):
        slot_of[assign[i]] = i
        return carry

    lax.fori_loop(0, assign.shape[0], body, 0)


def is_opening(span, counts):
    start, found = jnp.int32(0), jnp.int32(0)
    for k in range(counts.shape[0]):
        found = jnp.where(span == start, jnp.int32(1), found)
        start = start + counts[k]
    return found


def lay_out_taps(x_ref, prev, padded):
    padded[...] = jnp.zeros_like(padded)
    swap = swap_matrix(FRAMES, COLS)

    def tile(s, f, r):
        return x_ref[s, f, r] if f >= 0 else prev(s, f, r)

    for r in range(0, ROWS, 2):
        for kt in range(3):
            cols = [
                jnp.concatenate([tile(s, 2 * t - 2 + kt, rr) for s in range(SLOTS) for t in range(STEPS)], axis=0)
                for rr in (r, r + 1)
            ]
            turned = dot(swap, jnp.concatenate(cols, axis=1)).astype(BF)
            for n in range(2):
                part = turned[:, n * CIN : (n + 1) * CIN].reshape(COLS, FRAMES, CIN)
                padded[kt, r + n + 1, 1 : COLS + 1] = part


def tap_block(padded, taps):
    blocks = [
        padded[kt, h : h + ROWS, w : w + COLS].reshape(ROWS * COLS * FRAMES, CIN) for h, w in taps for kt in range(3)
    ]
    return jnp.concatenate(blocks, axis=1)


def tap_rows(kt, h, w):
    at = ((kt * 3 + h) * 3 + w) * CIN
    return slice(at, at + CIN)


def device_at(me, chip_bits, core_bit):
    return me ^ (2 * chip_bits + core_bit)


def conv_kernel(cells, me_ref, x_ref, w_ref, *refs):
    out_refs, (main_part, edge_part, padded, edge, x_in, w_in, sem) = refs[:-7], refs[-7:]
    copies = [pltpu.make_async_copy(x_ref, x_in, sem.at[0]), pltpu.make_async_copy(w_ref, w_in, sem.at[1])]
    for copy in copies:
        copy.start()
    x_ref, w_ref = x_in, w_in
    copies[0].wait()
    lay_out_taps(x_ref, lambda s, f, r: jnp.zeros((COLS, CIN), BF), padded)
    wide = SLOTS * COLS
    i, j = iota((3 * wide, wide), 0), iota((3 * wide, wide), 1)
    k = i % wide
    q = (k // (SLOTS * cells)) * cells + k % cells
    s = (k // cells) % SLOTS
    shift = ((j // COLS == s) & (j % COLS == q + i // wide - 1)).astype(F32).astype(BF)
    edge[0] = jnp.zeros_like(edge[0])
    edge[ROWS + 1] = jnp.zeros_like(edge[0])
    for r in range(ROWS):
        tails = jnp.concatenate(
            [jnp.concatenate([x_ref[s, f, r] for s in range(SLOTS)], axis=0) for f in (6, 7)], axis=1
        )
        edge[r + 1] = dot(shift, tails).astype(BF)
    copies[1].wait()
    total = None
    for taps in TAP_SETS:
        rows = jnp.concatenate([w_ref[tap_rows(kt, h, w), :] for h, w in taps for kt in range(3)], axis=0)
        term = dot(tap_block(padded, taps), rows)
        total = term if total is None else total + term
    main = cells * FRAMES
    main_part[...] = total.astype(BF).reshape(main_part.shape)
    carry = None
    for h, w in TAPS:
        rows = jnp.concatenate([w_ref[tap_rows(kt, h, w), :] for kt in range(2)], axis=0)
        part = edge[h : h + ROWS, w * wide : (w + 1) * wide, :].reshape(ROWS * wide, 2 * CIN)
        term = dot(part, rows)
        carry = term if carry is None else carry + term
    edge_part[...] = carry.astype(BF).reshape(edge_part.shape)
    me = me_ref[0]
    for k, ref in enumerate(out_refs):
        for c in range(2):
            to = device_at(me, k, c)
            ref[c, :main, :] = main_part[to]
            ref[c, main:, :] = edge_part[to]


def run_conv(me, frames, taps, ctx):
    cells = ROWS * COLS // ctx
    return pl.pallas_call(
        functools.partial(conv_kernel, cells),
        out_shape=[jax.ShapeDtypeStruct((2, cells * (FRAMES + SLOTS), COUT), BF)] * (ctx // 2),
        in_specs=[SMEM, HBM, HBM],
        out_specs=[VMEM] * (ctx // 2),
        scratch_shapes=[
            pltpu.VMEM((ctx, cells * FRAMES, COUT), BF),
            pltpu.VMEM((ctx, cells * SLOTS, COUT), BF),
            pltpu.VMEM(PADDED, BF),
            pltpu.VMEM((ROWS + 2, 3 * SLOTS * COLS, 2 * CIN), BF),
            pltpu.VMEM(frames.shape, BF),
            pltpu.VMEM(taps.shape, BF),
            pltpu.SemaphoreType.DMA((2,)),
        ],
        compiler_params=params(50),
        cost_estimate=cost(4_800_000_000, 4_000_000),
        name="conv_forward",
    )(me, frames, taps)


def tails_kernel(x_ref, out_ref, sem):
    copy = pltpu.make_async_copy(x_ref.at[:, 6:8], out_ref, sem)
    copy.start()
    copy.wait()


def run_tails(frames):
    return pl.pallas_call(
        tails_kernel,
        out_shape=jax.ShapeDtypeStruct((SLOTS, 2, ROWS, COLS, CIN), BF),
        in_specs=[HBM],
        out_specs=VMEM,
        scratch_shapes=[pltpu.SemaphoreType.DMA],
        compiler_params=params(4),
        cost_estimate=cost(0, 500_000),
        name="cut_tails",
    )(frames)


def grad_kernel(chips, assign, counts, me_ref, xs_ref, xo_ref, us_ref, uo_ref, *refs):
    tails, refs = refs[: 2 * chips], refs[2 * chips :]
    out_refs = refs[:chips]
    slot_of, padded, turned, product, before, sem = refs[chips:]
    fill_slots(assign, slot_of)
    me = me_ref[0]
    openings = []
    for core in range(2):
        for i in range(SLOTS):
            span = assign[(me ^ core) * SLOTS + i]
            openings.append(is_opening(span, counts))
            slot = slot_of[jnp.maximum(span - 1, 0)]
            apart = (slot // SLOTS) ^ me
            for n, ref in enumerate(tails):

                @pl.when(apart == n)
                def _():
                    at = core * SLOTS + i
                    pltpu.make_async_copy(ref.at[slot % SLOTS], before.at[at], sem.at[at]).start()

    for at in range(2 * SLOTS):
        pltpu.make_async_copy(tails[0].at[0], before.at[at], sem.at[at]).wait()

    swap = swap_matrix(FRAMES, COLS)
    span_rows = COLS * FRAMES
    total = ROWS * span_rows
    for core, (x_ref, u_ref) in enumerate(((xs_ref, us_ref), (xo_ref, uo_ref))):

        def prev(s, f, r):
            got = before[core * SLOTS + s, f + 2, r]
            return jnp.where(openings[core * SLOTS + s] > 0, jnp.zeros_like(got), got)

        lay_out_taps(x_ref, prev, padded.at[core])
        for r in range(ROWS):
            block = jnp.concatenate(
                [u_ref[s, t, r * COLS : (r + 1) * COLS, :] for s in range(SLOTS) for t in range(STEPS)], axis=0
            )
            at = core * total + r * span_rows
            turned[:, at : at + span_rows] = dot(swap, block).T.astype(BF)

    def entries(tap):
        kt, h, w = tap // 9, (tap // 3) % 3, tap % 3
        cores = [
            padded[core, kt, pl.ds(h, ROWS), pl.ds(w, COLS)].reshape(total, CIN) for core in range(2)
        ]
        return jnp.concatenate(cores, axis=0)

    rows = out_refs[0].shape[0]
    count = -(-rows // CIN)
    for k, ref in enumerate(out_refs):
        first = device_at(me, k, 0) * rows
        tap, offset = first // CIN, first % CIN
        near = jnp.concatenate([entries(jnp.minimum(tap + n, 26)) for n in range(count)], axis=1)
        product[: count * CIN, :] = dot(turned[...], near).T

        @pl.when(offset + rows > count * CIN)
        def _():
            product[count * CIN :, :] = dot(turned[...], entries(jnp.minimum(tap + count, 26))).T

        if rows % 16 == 0:
            ref[...] = product[pl.ds(pl.multiple_of(offset, 16), rows), :].astype(ref.dtype)
        else:
            size = product.shape[0]
            ref[...] = pltpu.roll(product[...], (size - offset) % size, 0)[:rows].astype(ref.dtype)


def run_grad(assign, counts, me, frames, upstream, tails, ctx):
    chips, rows = ctx // 2, 27 * CIN // ctx
    return pl.pallas_call(
        functools.partial(grad_kernel, chips),
        out_shape=[jax.ShapeDtypeStruct((rows, COUT), F32 if k == 0 else BF) for k in range(chips)],
        in_specs=[SMEM, SMEM, SMEM, VMEM, VMEM, VMEM, VMEM] + [ANY] * ctx,
        out_specs=[VMEM] * chips,
        scratch_shapes=[
            pltpu.SMEM(assign.shape, jnp.int32),
            pltpu.VMEM((2,) + PADDED, BF),
            pltpu.VMEM((COUT, 2 * ROWS * COLS * FRAMES), BF),
            pltpu.VMEM(((-(-rows // CIN) + 1) * CIN, COUT), F32),
            pltpu.VMEM((2 * SLOTS, 2, ROWS, COLS, CIN), BF),
            pltpu.SemaphoreType.DMA((2 * SLOTS,)),
        ],
        compiler_params=params(32),
        cost_estimate=cost(1000, 1000),
        name="conv_gradient",
    )(assign, counts, me, *frames, *upstream, *tails)


def attend_kernel(cells, ctx, assign, counts, scale, me_ref, qkv_ref, last_ref, *refs):
    chips = ctx // 2
    got_refs, out_refs = refs[:ctx], refs[ctx : ctx + chips]
    slot_of, rows_of, q_ref, k_ref, v_ref, edges, bias = refs[ctx + chips :]
    me = me_ref[0]
    main = cells * FRAMES
    total = ctx * FRAMES
    block = min(128, total)
    fill_slots(assign, slot_of)

    def mark(shape, axis):
        spot = iota(shape, axis)
        span = jnp.zeros(shape, jnp.int32)
        for i in range(ctx * SLOTS):
            span = jnp.where(spot // STEPS == i, assign[(me ^ (i // SLOTS)) * SLOTS + i % SLOTS], span)
        clip, end = jnp.zeros(shape, jnp.int32), jnp.int32(0)
        for k in range(counts.shape[0]):
            end = end + counts[k]
            clip = clip + (span >= end).astype(jnp.int32)
        return span * STEPS + spot % STEPS, clip

    time_b, clip_b = mark((1, total), 1)
    time_a, clip_a = mark((total, 1), 0)
    allowed = (clip_a == clip_b) & (time_b <= time_a)
    bias[...] = jnp.where(allowed, 0.0, -1e30)

    i, j = iota((main, main), 0), iota((main, main), 1)
    held = j // (SLOTS * cells)
    fits = (i % STEPS == 0) & ((i // STEPS) % SLOTS == held) & (i // FRAMES == j % cells)
    base = jnp.where(fits, 1, 0)
    lane = iota((1, main), 1)
    from_slot = (lane // cells) % SLOTS
    lane_held = lane // (SLOTS * cells)
    same_head = (iota((COUT, COUT), 0) // 64 == iota((COUT, COUT), 1) // 64).astype(F32).astype(BF)
    head = iota((1, COUT), 1) // 64
    gain = jnp.zeros((1, COUT), F32)
    for h in range(COUT // 64):
        gain = jnp.where(head == h, scale[h], gain)

    for src in range(ctx):
        edges[src] = got_refs[src][0, main:, :]
        rows_of[src] = got_refs[src][0, :main, :].reshape(cells, FRAMES, COUT)

    def project(src, carry):
        pick = jnp.full((1, main), -1, jnp.int32)
        blocks = []
        for s in range(SLOTS):
            span = assign[(me ^ src) * SLOTS + s]
            slot = slot_of[jnp.maximum(span - 1, 0)]
            spot = jnp.where(is_opening(span, counts) > 0, -1, slot % SLOTS)
            pick = jnp.where(lane_held == s, spot, pick)
            blocks.append(edges[(slot // SLOTS) ^ me])
        chosen = jnp.where(pick == from_slot, base, 0).astype(F32).astype(BF)
        value = rows_of[src].reshape(main, COUT).astype(F32) + dot(chosen, jnp.concatenate(blocks, axis=0))
        value = value.astype(BF)
        rows_of[src] = value.reshape(cells, FRAMES, COUT)
        value = value.astype(F32)
        normed = value * lax.rsqrt(jnp.mean(value * value, axis=-1, keepdims=True) + 1e-6)
        mapped = dot(normed.astype(BF), qkv_ref[...])
        query, key = mapped[:, :COUT], mapped[:, COUT : 2 * COUT]
        query = query * (lax.rsqrt(dot((query * query).astype(BF), same_head) + 1e-6) * gain)
        key = key * lax.rsqrt(dot((key * key).astype(BF), same_head) + 1e-6)
        q_ref[src] = query.astype(BF).reshape(cells, FRAMES, COUT)
        k_ref[src] = key.astype(BF).reshape(cells, FRAMES, COUT)
        v_ref[src] = mapped[:, 2 * COUT :].astype(BF).reshape(cells, FRAMES, COUT)
        return carry

    lax.fori_loop(0, ctx, project, 0, unroll=8 if total == block else 1)

    low = iota((1, 128), 1) < 64
    ones = [jnp.where(low, 1.0, 0.0), jnp.where(low, 0.0, 1.0)]

    def mix(cell, carry):
        for pair in range(2):
            lanes = slice(pair * 128, (pair + 1) * 128)
            key = k_ref[:, cell, :, lanes].reshape(total, 128)
            value = v_ref[:, cell, :, lanes].reshape(total, 128)
            zero = jnp.zeros_like(key)
            keys = jnp.concatenate([jnp.where(low, key, zero), jnp.where(low, zero, key)], axis=0)
            sides = [jnp.where(low, value, zero), jnp.where(low, zero, value)]
            flags = [jnp.broadcast_to(ones[n].astype(BF), (total, 128)) for n in range(2)]
            values = jnp.concatenate(
                [jnp.concatenate([sides[n], flags[n]], axis=1) for n in range(2)], axis=0
            )
            for at in range(0, total, block):
                part = slice(at // FRAMES, (at + block) // FRAMES)
                query = q_ref[part, cell, :, lanes].reshape(block, 128)
                logits = dot_t(query, keys)
                mask = bias[at : at + block, :]
                weights = jnp.exp(logits + jnp.concatenate([mask, mask], axis=1)).astype(BF)
                sums = dot(weights, values)
                mixed = (sums[:, :128] / sums[:, 128:]).astype(BF)
                q_ref[part, cell, :, lanes] = mixed.reshape(block // FRAMES, FRAMES, 128)
        return carry

    lax.fori_loop(0, cells, mix, 0, unroll=cells if total == block else 1)

    turn = swap_matrix(cells, FRAMES)

    for src in range(ctx):
        mixed = q_ref[src].reshape(main, COUT)
        value = rows_of[src].reshape(main, COUT).astype(F32)
        latent = (value + dot(mixed, last_ref[...])).astype(BF)
        out_refs[src // 2][src % 2] = dot(turn, latent).astype(BF)


def run_attend(assign, counts, scale, me, got, qkv, last, ctx):
    cells = ROWS * COLS // ctx
    total = ctx * FRAMES
    held = pltpu.VMEM((ctx, cells, FRAMES, COUT), BF)
    piece = (1, cells * (FRAMES + SLOTS), COUT)

    def whole(array):
        return pl.BlockSpec(array.shape, lambda i: (0,) * array.ndim)

    def half(n):
        return pl.BlockSpec(piece, lambda i: (n, 0, 0))

    out = (2, cells * FRAMES, COUT)
    return pl.pallas_call(
        functools.partial(attend_kernel, cells, ctx),
        grid=(1,),
        out_shape=[jax.ShapeDtypeStruct(out, BF)] * (ctx // 2),
        in_specs=[SMEM, SMEM, SMEM, SMEM, whole(qkv), whole(last)] + [half(n % 2) for n in range(ctx)],
        out_specs=[pl.BlockSpec(out, lambda i: (0, 0, 0))] * (ctx // 2),
        scratch_shapes=[
            pltpu.SMEM(assign.shape, jnp.int32),
            held,
            held,
            held,
            held,
            pltpu.VMEM((ctx, cells * SLOTS, COUT), BF),
            pltpu.VMEM((total, total), F32),
        ],
        compiler_params=params(24),
        cost_estimate=cost(1000, 1000),
        name="attend",
    )(assign, counts, scale, me, qkv, last, *got)


def place_kernel(me_ref, *refs):
    out_ref = refs[-1]
    for n, ref in enumerate(refs[:-1]):
        out_ref[:, me_ref[0] ^ n] = ref[0]


def run_place(me, pieces, ctx):
    cells = ROWS * COLS // ctx
    pieces = [piece.reshape(2, FRAMES, cells, COUT) for piece in pieces]
    shape = (FRAMES, ctx, cells, COUT)

    def half(n):
        return pl.BlockSpec((1,) + pieces[0].shape[1:], lambda i: (n, 0, 0, 0))

    return pl.pallas_call(
        place_kernel,
        grid=(1,),
        out_shape=jax.ShapeDtypeStruct(shape, BF),
        in_specs=[SMEM] + [half(n % 2) for n in range(ctx)],
        out_specs=pl.BlockSpec(shape, lambda i: (0, 0, 0, 0)),
        compiler_params=params(8),
        cost_estimate=cost(0, 2_000_000),
        name="place_latents",
    )(me, *pieces)


def flip(value, axis, size, bits):
    return lax.ppermute(value, axis, [(i, i ^ bits) for i in range(size)])


def send_far(parts, ctx):
    far = [parts[0]] + [None] * (len(parts) - 1)
    for k in reversed(range(1, len(parts))):
        far[k] = flip(parts[k], "ctx", ctx, 2 * k)
    return far


def send_near(value, ctx):
    return flip(value, "ctx", ctx, 1)


def hold(values, after):
    return lax.optimization_barrier((values, after))[0]


def weave(far, near):
    return [piece for pair in zip(far, near) for piece in pair]


def per_device(ctx, dp, frames, assign, counts, scale, taps, qkv, last, upstream):
    me = lax.axis_index("ctx").astype(jnp.int32).reshape(1)
    frames, upstream = frames[0], upstream[0]
    cells = ROWS * COLS // ctx
    chips = ctx // 2
    both_frames = (frames, send_near(frames, ctx))
    both_upstream = (upstream, send_near(upstream, ctx))
    tails = send_far([run_tails(frames)] * chips, ctx)
    sent = run_conv(me, frames, taps, ctx)
    got = send_far(sent, ctx)

    tails = hold(tails, sent[0])
    tails = weave(tails, [send_near(part, ctx) for part in tails])
    halves = run_grad(assign, counts, me, both_frames, both_upstream, tails, ctx)
    got = [got[0]] + hold(got[1:], halves[1:])
    got_near = [send_near(part, ctx) for part in got]
    moved = [flip(halves[k], "ctx", ctx, 2 * k) for k in range(1, chips)]
    blended = run_attend(assign, counts, scale, me, weave(got, got_near), qkv, last, ctx)
    share = halves[0]
    for part in hold(moved, blended[0]):
        share = share + part.astype(F32)
    back = send_far(blended, ctx)
    bits = 1
    while bits < dp:
        share = share.astype(BF)
        share = share.astype(F32) + flip(share, "dp", dp, bits).astype(F32)
        bits *= 2
    latents = run_place(me, weave(back, [send_near(part, ctx) for part in back]), ctx)
    return (latents.reshape(1, SLOTS, STEPS, ctx * cells, COUT), share)


def solution(mesh):
    placed = (
        P("dp", "ctx", None, None, None, None),
        P(),
        P(),
        P(),
        P(),
        P(),
        P(),
        P("dp", "ctx", None, None, None),
    )
    return jax.shard_map(
        functools.partial(per_device, mesh.shape["ctx"], mesh.shape["dp"]),
        mesh=mesh,
        in_specs=placed,
        out_specs=(P("dp", "ctx", None, None, None), P("ctx", None)),
        check_vma=False,
    )
```
